512 devices in a mesh: dp: 64 (over y_hi, z, core), tensor: 8 (over y_lo, x).
Axes of the slice: x: 4, y: 4 (y_hi: 2, y_lo: 2; y = y_hi * 2 + y_lo), z: 16, core: 2. Of those that a mesh axis runs over, the one named last changes fastest.
Arguments:
- tokens: bfloat16 [512, 8192], P('dp', 'tensor'), may hold values from -6 to 6
- gate_weight: bfloat16 [8192, 16384], P('tensor', 'dp'), may hold values from -0.125 to 0.125
- up_weight: bfloat16 [8192, 16384], P('tensor', 'dp'), may hold values from -0.125 to 0.125
- down_weight: bfloat16 [16384, 8192], P('dp', 'tensor'), may hold values from -0.09375 to 0.09375
- gate_mask: int32 [64, 128], P('tensor', 'dp'), may hold values 0 or 1
- up_mask: int32 [64, 128], P('tensor', 'dp'), may hold values 0 or 1
- down_mask: int32 [128, 64], P('dp', 'tensor'), may hold values 0 or 1
- probe_gate: bfloat16 [8192, 16384], P('tensor', 'dp'), may hold values from -1 to 1, as said below
- probe_up: bfloat16 [8192, 16384], P('tensor', 'dp'), may hold values from -1 to 1, as said below
- probe_down: bfloat16 [16384, 8192], P('dp', 'tensor'), may hold values from -1 to 1, as said below
Outputs:
- fisher_gate: bfloat16 [8192, 16384], P('tensor', 'dp')
- fisher_up: bfloat16 [8192, 16384], P('tensor', 'dp')
- fisher_down: bfloat16 [16384, 8192], P('dp', 'tensor')
The draws below stay inside these ranges and needn't reach their ends.
Inputs may be any that keep to these rules, and one draw needn't show every extreme that they name: `probe_gate`: every entry is -1 or +1. `probe_up`: every entry is -1 or +1. `probe_down`: every entry is -1 or +1.
All inputs are finite; a program needn't handle non-finite values. No bound on the sum of `gate_mask` or of `up_mask` or of `down_mask` on one device may be relied on, other than what follows from the above.
Results may differ from the reference program's by a relative error of at most 0.008.
Values may be sent and summed in bfloat16 or wider, within the bound.
No kernel may reach another device: no remote copies, remote signals or barrier semaphores. Data moves between devices by JAX's collectives and lax.ppermute only.
A program may use at most 64 MiB of HBM per device.

```python
import jax
import jax.numpy as jnp

D = 8192
HID = 16384
BLOCK = 128
TOKENS = 512


def draw_probe_gate(key, part):
    key = jax.random.fold_in(key, 11)
    return jax.random.rademacher(key, (D, HID), jnp.float32).astype(jnp.bfloat16)


def draw_probe_up(key, part):
    key = jax.random.fold_in(key, 23)
    return jax.random.rademacher(key, (D, HID), jnp.float32).astype(jnp.bfloat16)


def draw_probe_down(key, part):
    key = jax.random.fold_in(key, 37)
    return jax.random.rademacher(key, (HID, D), jnp.float32).astype(jnp.bfloat16)


def touch_ends(values, stream_key, low, high):
    spot = [jax.random.randint(jax.random.fold_in(stream_key, axis), (), 0, length) for axis, length in enumerate(values.shape)]
    main_axis = values.shape.index(max(values.shape))
    neighbour = spot[:main_axis] + [(spot[main_axis] + 1) % values.shape[main_axis]] + spot[main_axis + 1:]
    return values.at[tuple(spot)].set(low).at[tuple(neighbour)].set(high)


def block_levels(key, extent, cuts, smallest, largest):
    factor_of = 1.0
    for dim, blocks in cuts:
        draws = jax.random.uniform(jax.random.fold_in(jax.random.fold_in(key, 6), dim), (blocks,), jnp.float32, smallest / len(cuts), largest / len(cuts))
        factor_of = factor_of * jnp.repeat(jnp.exp(draws), extent[dim] // blocks).reshape((-1,) + (1,) * (len(extent) - 1 - dim))
    return factor_of


def centred(own_key, shape, spread, bound, pieces=(), held_as=jnp.bfloat16):
    array = jax.random.normal(own_key, shape, jnp.float32) * spread
    if len(pieces) > 0:
        array = block_levels(own_key, shape, pieces, -0.22, 0.18) * array
    return jnp.clip(array, min=-bound, max=bound).astype(held_as)


def setup_inputs(seed: int = 0) -> dict:
    seeds = jax.random.split(jax.random.key(seed), 11)
    tokens = centred(seeds[0], (TOKENS, D), 1.0, 6.0, ((0, 64), (1, 8)))
    gate_weight = centred(seeds[1], (D, HID), (D // 4) ** -0.5, 0.125, ((0, 8), (1, 64)))
    up_weight = centred(seeds[2], (D, HID), (D // 4) ** -0.5, 0.125, ((0, 8), (1, 64)))
    down_weight = centred(seeds[3], (HID, D), (HID // 4) ** -0.5, 0.09375, ((0, 64), (1, 8)))
    gate_mask = touch_ends((jax.random.randint(seeds[4], (D // BLOCK, HID // BLOCK), 0, 4) < 1).astype(jnp.int32), jax.random.fold_in(seeds[4], 1), 0, 1)
    up_mask = touch_ends((jax.random.randint(seeds[5], (D // BLOCK, HID // BLOCK), 0, 4) < 1).astype(jnp.int32), jax.random.fold_in(seeds[5], 1), 0, 1)
    down_mask = touch_ends((jax.random.randint(seeds[6], (HID // BLOCK, D // BLOCK), 0, 4) < 1).astype(jnp.int32), jax.random.fold_in(seeds[6], 1), 0, 1)
    probe_gate = draw_probe_gate(jax.random.fold_in(seeds[10], 71), 0)
    probe_up = draw_probe_up(jax.random.fold_in(seeds[10], 71), 0)
    probe_down = draw_probe_down(jax.random.fold_in(seeds[10], 71), 0)
    return dict(tokens=tokens, gate_weight=gate_weight, up_weight=up_weight, down_weight=down_weight, gate_mask=gate_mask, up_mask=up_mask, down_mask=down_mask, probe_gate=probe_gate, probe_up=probe_up, probe_down=probe_down)


def widen(mask):
    grown = jnp.repeat(jnp.repeat(mask, BLOCK, axis=0), BLOCK, axis=1)
    return grown.astype(jnp.bfloat16)


def reference(tokens, gate_weight, up_weight, down_weight, gate_mask, up_mask, down_mask, probe_gate, probe_up, probe_down):
    kept_gate = gate_weight * widen(gate_mask)
    kept_up = up_weight * widen(up_mask)
    kept_down = down_weight * widen(down_mask)
    gate = jnp.dot(tokens, kept_gate, preferred_element_type=jnp.float32)
    up = jnp.dot(tokens, kept_up, preferred_element_type=jnp.float32)
    tangent_gate = jnp.dot(tokens, probe_gate, preferred_element_type=jnp.float32) * (D ** -0.5)
    tangent_up = jnp.dot(tokens, probe_up, preferred_element_type=jnp.float32) * (D ** -0.5)
    sig = jax.nn.sigmoid(gate)
    act = gate * sig
    slope = sig * (1.0 + gate * (1.0 - sig))
    hidden = (act * up).astype(jnp.bfloat16)
    tangent_hidden = (slope * tangent_gate * up + act * tangent_up).astype(jnp.bfloat16)
    tangent_out = jnp.dot(tangent_hidden, kept_down, preferred_element_type=jnp.float32)
    tangent_out = tangent_out + jnp.dot(hidden, probe_down, preferred_element_type=jnp.float32) * (HID ** -0.5)
    tangent_out = tangent_out.astype(jnp.bfloat16)
    back = jnp.dot(tangent_out, kept_down.T, preferred_element_type=jnp.float32)
    gate_bar = (back * up * slope).astype(jnp.bfloat16)
    up_bar = (back * act).astype(jnp.bfloat16)
    factor = TOKENS ** -0.5
    grad_gate = jnp.dot(tokens.T, gate_bar, preferred_element_type=jnp.float32)
    grad_up = jnp.dot(tokens.T, up_bar, preferred_element_type=jnp.float32)
    grad_down = jnp.dot(hidden.T, tangent_out, preferred_element_type=jnp.float32)
    fisher_gate = (probe_gate.astype(jnp.float32) * grad_gate * factor).astype(jnp.bfloat16)
    fisher_up = (probe_up.astype(jnp.float32) * grad_up * factor).astype(jnp.bfloat16)
    fisher_down = (probe_down.astype(jnp.float32) * grad_down * factor).astype(jnp.bfloat16)
    return (fisher_gate, fisher_up, fisher_down)
```

```python
import jax
import jax.numpy as jnp
from jax import lax
from jax.sharding import Mesh, PartitionSpec as P

D = 8192
HID = 16384
BF16 = jnp.bfloat16
F32 = jnp.float32
DP = ("yh", "z", "c")
TP = ("yl", "x")


def kept(weight, mask):
    rows, cols = weight.shape
    wide = jnp.repeat(mask.astype(BF16), cols // mask.shape[1], axis=1)
    blocks = weight.reshape(mask.shape[0], rows // mask.shape[0], cols)
    return (blocks * wide[:, None, :]).reshape(rows, cols)


def swap(x, axis):
    return lax.ppermute(x, axis, [(0, 1), (1, 0)])


def spread(x, axes, n):
    copies = jnp.broadcast_to(x[None], (n,) + x.shape)
    out = lax.all_to_all(copies, axes, 0, 0, tiled=True)
    return out.reshape((n * x.shape[0],) + x.shape[1:])


def scatter_sum(x, axes, n):
    pieces = x.reshape((n, x.shape[0] // n) + x.shape[1:])
    out = lax.all_to_all(pieces, axes, 0, 0, tiled=True)
    return jnp.sum(out.astype(F32), axis=0)


def gather_dp(x):
    x = spread(x, "z", 16)
    x = jnp.concatenate([x, swap(x, "yh")], axis=0)
    return jnp.concatenate([x, swap(x, "c")], axis=0)


def fold(x, axis):
    half = x.shape[0] // 2
    return x[:half] + swap(x[half:].astype(BF16), axis).astype(F32)


def on_device(
    tokens,
    gate_weight,
    up_weight,
    down_weight,
    gate_mask,
    up_mask,
    down_mask,
    probe_gate,
    probe_up,
    probe_down,
):
    width = gate_weight.shape[1]
    gathered = gather_dp(tokens)
    kept_gate = kept(gate_weight, gate_mask)
    kept_up = kept(up_weight, up_mask)
    kept_down = kept(down_weight, down_mask)
    stacked = jnp.concatenate([kept_gate, kept_up, probe_gate, probe_up], axis=1)
    partial = jnp.dot(gathered, stacked, preferred_element_type=F32).astype(BF16)
    pre = scatter_sum(partial, TP, 8)
    gate = pre[:, :width]
    up = pre[:, width : 2 * width]
    tangent_gate = pre[:, 2 * width : 3 * width] * D**-0.5
    tangent_up = pre[:, 3 * width :] * D**-0.5
    sig = jax.nn.sigmoid(gate)
    act = gate * sig
    slope = sig * (1.0 + gate * (1.0 - sig))
    hid = (act * up).astype(BF16)
    tan = (slope * tangent_gate * up + act * tangent_up).astype(BF16)
    both = spread(jnp.concatenate([tan, hid], axis=1), TP, 8)
    hidden = both[:, width:]
    down = jnp.concatenate([kept_down, probe_down * HID**-0.5], axis=0)
    term = jnp.dot(both, down, preferred_element_type=F32)
    term = fold(term, "c")
    term = fold(term, "yh")
    chunk = scatter_sum(term.astype(BF16), "z", 16).astype(BF16)
    tangent_out = gather_dp(chunk)
    back = lax.dot_general(
        tangent_out, kept_down, (((1,), (1,)), ((), ())), preferred_element_type=F32
    )
    back = scatter_sum(back.astype(BF16), TP, 8)
    bars = jnp.concatenate([(back * up * slope).astype(BF16), (back * act).astype(BF16)], axis=1)
    bars = spread(bars, TP, 8)
    factor = gathered.shape[0] ** -0.5
    contract = (((0,), (0,)), ((), ()))
    grads = lax.dot_general(gathered, bars, contract, preferred_element_type=F32)
    grad_down = lax.dot_general(hidden, tangent_out, contract, preferred_element_type=F32)
    fisher_gate = (probe_gate.astype(F32) * grads[:, :width] * factor).astype(BF16)
    fisher_up = (probe_up.astype(F32) * grads[:, width:] * factor).astype(BF16)
    fisher_down = (probe_down.astype(F32) * grad_down * factor).astype(BF16)
    return (fisher_gate, fisher_up, fisher_down)


def solution(mesh):
    fine = Mesh(mesh.devices.reshape(2, 16, 2, 2, 4), DP + TP)
    col = P(TP, DP)
    row = P(DP, TP)
    return jax.shard_map(
        on_device,
        mesh=fine,
        in_specs=(row, col, col, row, col, col, row, col, col, row),
        out_specs=(col, col, row),
        check_vma=False,
    )
```

```python
import jax
import jax.numpy as jnp
from jax import lax
from jax.sharding import Mesh, PartitionSpec as P

D = 8192
HID = 16384
BF16 = jnp.bfloat16
F32 = jnp.float32
DP = ("yh", "zh", "zl", "c")
TP = ("yl", "x")


def kept(weight, mask):
    rows, cols = weight.shape
    wide = jnp.repeat(mask.astype(BF16), cols // mask.shape[1], axis=1)
    blocks = weight.reshape(mask.shape[0], rows // mask.shape[0], cols)
    return (blocks * wide[:, None, :]).reshape(rows, cols)


def swap(x, axis):
    return lax.ppermute(x, axis, [(0, 1), (1, 0)])


def exchange(pieces, axes):
    return lax.all_to_all(pieces, axes, 0, 0, tiled=True)


def copies(x, n):
    return jnp.broadcast_to(x[None], (n,) + x.shape)


def total(pieces):
    return jnp.sum(pieces.astype(F32), axis=0)


def own_first(x, axis):
    return jnp.where(lax.axis_index(axis) == 0, x, x[::-1])


def split_rows(x, own):
    first = x[:own].reshape((8, own // 8) + x.shape[1:])
    rest = x[own:].reshape((8, -1) + x.shape[1:])
    return jnp.concatenate([first, rest], axis=1)


def join_rows(x, own):
    first = x[:, : own // 8].reshape((own,) + x.shape[2:])
    rest = x[:, own // 8 :].reshape((-1,) + x.shape[2:])
    return jnp.concatenate([first, rest], axis=0)


def on_device(
    tokens,
    gate_weight,
    up_weight,
    down_weight,
    gate_mask,
    up_mask,
    down_mask,
    probe_gate,
    probe_up,
    probe_down,
):
    width = gate_weight.shape[1]
    feats = tokens.shape[1]
    kept_gate = kept(gate_weight, gate_mask)
    kept_up = kept(up_weight, up_mask)
    kept_down = kept(down_weight, down_mask)
    stacked = jnp.concatenate([kept_gate, kept_up, probe_gate, probe_up], axis=1)
    down = jnp.concatenate([kept_down, probe_down * HID**-0.5], axis=0)

    tok0 = exchange(copies(tokens, 16), ("zl", "zh")).reshape(128, feats)
    own = tok0.shape[0]
    tok1 = swap(tok0, "yh")
    pre0 = jnp.dot(tok0, stacked, preferred_element_type=F32).astype(BF16)
    pre0 = total(exchange(pre0.reshape(8, own // 8, 4 * width), TP))
    tok1, pre0 = lax.optimization_barrier((tok1, pre0))
    tok01 = jnp.concatenate([tok0, tok1], axis=0)
    tok23 = swap(tok01, "c")
    rest = jnp.concatenate([tok1, tok23], axis=0)
    pre1 = jnp.dot(rest, stacked, preferred_element_type=F32).astype(BF16)
    pre1 = total(exchange(pre1.reshape(8, -1, 4 * width), TP))
    gathered = jnp.concatenate([tok01, tok23], axis=0)
    shuffled = split_rows(gathered, own).reshape(gathered.shape)

    pre = jnp.concatenate([pre0, pre1], axis=0)
    gate = pre[:, :width]
    up = pre[:, width : 2 * width]
    tangent_gate = pre[:, 2 * width : 3 * width] * D**-0.5
    tangent_up = pre[:, 3 * width :] * D**-0.5
    sig = jax.nn.sigmoid(gate)
    act = gate * sig
    slope = sig * (1.0 + gate * (1.0 - sig))
    hid = (act * up).astype(BF16)
    tan = (slope * tangent_gate * up + act * tangent_up).astype(BF16)
    both = exchange(copies(jnp.concatenate([tan, hid], axis=1), 8), TP)
    hidden = both[:, :, width:].reshape(-1, width)
    both = join_rows(both, own)

    half = both.shape[0] // 2
    away = jnp.dot(both[half:], down, preferred_element_type=F32).astype(BF16)
    away = swap(away, "c")
    term = jnp.dot(both[:half], down, preferred_element_type=F32) + away.astype(F32)
    term = own_first(term.astype(BF16).reshape(2, 4, 32, feats), "yh")
    term = exchange(term.transpose(1, 0, 2, 3).reshape(8, 32, feats), ("zl", "yh"))
    chunk = total(term).astype(BF16)
    chunk = total(exchange(copies(chunk, 4), "zh")).astype(BF16)
    out01 = exchange(copies(chunk, 8), ("zl", "yh")).reshape(4, 2, 32, feats)
    out01 = own_first(out01.transpose(1, 0, 2, 3), "yh").reshape(half, feats)
    out23 = swap(out01, "c")
    tangent_out = jnp.concatenate([out01, out23], axis=0)

    back = lax.dot_general(
        tangent_out, kept_down, (((1,), (1,)), ((), ())), preferred_element_type=F32
    )
    back = total(exchange(split_rows(back.astype(BF16), own), TP))
    bars = jnp.concatenate([(back * up * slope).astype(BF16), (back * act).astype(BF16)], axis=1)
    bars = exchange(copies(bars, 8), TP).reshape(gathered.shape[0], 2 * width)
    factor = gathered.shape[0] ** -0.5
    contract = (((0,), (0,)), ((), ()))
    out_shuffled = split_rows(tangent_out, own).reshape(gathered.shape)
    grad_down = lax.dot_general(hidden, out_shuffled, contract, preferred_element_type=F32)
    grads = lax.dot_general(shuffled, bars, contract, preferred_element_type=F32)
    fisher_gate = (probe_gate.astype(F32) * grads[:, :width] * factor).astype(BF16)
    fisher_up = (probe_up.astype(F32) * grads[:, width:] * factor).astype(BF16)
    fisher_down = (probe_down.astype(F32) * grad_down * factor).astype(BF16)
    return (fisher_gate, fisher_up, fisher_down)


def solution(mesh):
    fine = Mesh(mesh.devices.reshape(2, 4, 4, 2, 2, 4), DP + TP)
    col = P(TP, DP)
    row = P(DP, TP)
    return jax.shard_map(
        on_device,
        mesh=fine,
        in_specs=(row, col, col, row, col, col, row, col, col, row),
        out_specs=(col, col, row),
        check_vma=False,
    )
```

```python
import jax
import jax.numpy as jnp
from jax import lax
from jax.sharding import Mesh, PartitionSpec as P

D = 8192
HID = 16384
BF16 = jnp.bfloat16
F32 = jnp.float32
DP = ("yh", "zh", "zl", "c")
TP = ("yl", "x")
NEAR = ("yh", "c", "yl", "x")


def kept(weight, mask):
    rows, cols = weight.shape
    wide = jnp.repeat(mask.astype(BF16), cols // mask.shape[1], axis=1)
    blocks = weight.reshape(mask.shape[0], rows // mask.shape[0], cols)
    return (blocks * wide[:, None, :]).reshape(rows, cols)


def swap(x, axis):
    return lax.ppermute(x, axis, [(0, 1), (1, 0)])


def step_y(x, way):
    return lax.ppermute(x, ("yh", "yl"), [(i, (i + way) % 4) for i in range(4)])


def exchange(pieces, axes):
    return lax.all_to_all(pieces, axes, 0, 0, tiled=True)


def together(arrays):
    return lax.optimization_barrier(arrays)


def copies(x, n):
    return jnp.broadcast_to(x[None], (n,) + x.shape)


def total(pieces, axis=0):
    return jnp.sum(pieces.astype(F32), axis=axis)


def reorder(x):
    x = jnp.where(lax.axis_index("c") == 0, x, x[:, ::-1])
    return jnp.where(lax.axis_index("yh") == 0, x, x[::-1])


def by_position(own, over_c, over_y, over_both):
    x = reorder(jnp.stack([own, over_c, over_y, over_both]).reshape((2, 2) + own.shape))
    return x.reshape((4 * own.shape[0],) + own.shape[1:])


def dot(a, b, dims=((1,), (0,))):
    return lax.dot_general(a, b, (dims, ((), ())), preferred_element_type=F32)


def on_device(
    tokens,
    gate_weight,
    up_weight,
    down_weight,
    gate_mask,
    up_mask,
    down_mask,
    probe_gate,
    probe_up,
    probe_down,
):
    width = gate_weight.shape[1]
    feats = tokens.shape[1]

    tok0 = exchange(copies(tokens, 16), ("zl", "zh")).reshape(8, 16, feats)
    kept_down = kept(down_weight, down_mask)
    kept_gate = kept(gate_weight, gate_mask)
    kept_up = kept(up_weight, up_mask)
    kept_c, probe_c = swap(kept_down, "c"), swap(probe_down, "c")
    kept_y, probe_y = step_y(kept_down, 1), step_y(probe_down, -1)
    tok0, kept_gate, kept_up, kept_c, probe_c, kept_y, probe_y = together(
        (tok0, kept_gate, kept_up, kept_c, probe_c, kept_y, probe_y)
    )
    stacked = jnp.concatenate([kept_gate, kept_up, probe_gate, probe_up], axis=1)

    tok1 = swap(tok0, "yh")
    pair = jnp.stack([tok0, tok1], axis=1)
    other = swap(pair, "c")
    gathered = jnp.stack([pair, other], axis=2).reshape(-1, feats)
    partial = dot(gathered, stacked).astype(BF16)
    partial, kept_y, probe_y = together((partial, kept_y, probe_y))
    pre = exchange(partial.reshape(8, -1, 4 * width), TP)
    pre, kept_y, probe_y = together((pre, step_y(kept_y, 1), step_y(probe_y, -1)))
    pre = total(pre)

    gate = pre[:, :width]
    up = pre[:, width : 2 * width]
    tangent_gate = pre[:, 2 * width : 3 * width] * D**-0.5
    tangent_up = pre[:, 3 * width :] * D**-0.5
    sig = jax.nn.sigmoid(gate)
    act = gate * sig
    slope = sig * (1.0 + gate * (1.0 - sig))
    hid = (act * up).astype(BF16)
    tan = (slope * tangent_gate * up + act * tangent_up).astype(BF16)
    both = jnp.concatenate([tan, hid], axis=1).reshape(2, 2, 16, 2 * width)
    both = reorder(both).reshape(4, 1, 16, 2 * width)
    both = jnp.broadcast_to(both, (4, 8, 16, 2 * width)).reshape(32, 16, 2 * width)
    both, kept_y, probe_y = together((both, kept_y, probe_y))
    both = exchange(both, NEAR).reshape(4, 128, 2 * width)
    kept4 = by_position(kept_down, kept_c, kept_y, swap(kept_y, "c"))
    probe4 = by_position(probe_down, probe_c, probe_y, swap(probe_y, "c"))
    both, kept4, probe4 = together((both, kept4, probe4))
    tan4 = jnp.concatenate([both[i, :, :width] for i in range(4)], axis=1)
    hid4 = jnp.concatenate([both[i, :, width:] for i in range(4)], axis=1)

    term = dot(tan4, kept4) + dot(hid4, probe4) * HID**-0.5
    term, both = together((term.astype(BF16), both))
    mine = reorder(both[:, :, width:].reshape(2, 2, 128, width))
    term = exchange(term.reshape(4, 32, feats), "zl")
    term, mine = together((term, jnp.stack([mine[:, 0], swap(mine[:, 1], "c")])))
    chunk = exchange(copies(total(term).astype(BF16), 4), "zh")
    chunk, hidden = together((chunk, jnp.stack([mine[:, 0], swap(mine[:, 1], "yh")], axis=1)))
    hidden = hidden.reshape(-1, width)
    chunk = exchange(copies(total(chunk).astype(BF16), 4), "zl")
    out0 = chunk.reshape(128, feats)

    back = dot(out0, kept4, ((1,), (1,))).astype(BF16)
    back = jnp.stack([back[:, i * width : (i + 1) * width] for i in range(4)])
    back, out0 = together((back, out0))
    back = exchange(back.reshape(32, 16, width), NEAR)
    back, out1 = together((back, jnp.stack([out0, swap(out0, "yh")])))
    back = total(back.reshape(4, 8, 16, width), 1).reshape(2, 2, 16, width)
    back = reorder(back).reshape(64, width)
    bars = jnp.concatenate([(back * up * slope).astype(BF16), (back * act).astype(BF16)], axis=1)
    bars, out1 = together((bars, out1))
    bars = exchange(copies(bars, 8), TP).reshape(gathered.shape[0], 2 * width)
    tangent_out = jnp.stack([out1, swap(out1, "c")]).reshape(gathered.shape)

    factor = gathered.shape[0] ** -0.5
    grad_down = dot(hidden, tangent_out, ((0,), (0,)))
    grads = dot(gathered, bars, ((0,), (0,)))
    fisher_gate = (probe_gate.astype(F32) * grads[:, :width] * factor).astype(BF16)
    fisher_up = (probe_up.astype(F32) * grads[:, width:] * factor).astype(BF16)
    fisher_down = (probe_down.astype(F32) * grad_down * factor).astype(BF16)
    return (fisher_gate, fisher_up, fisher_down)


def solution(mesh):
    fine = Mesh(mesh.devices.reshape(2, 4, 4, 2, 2, 4), DP + TP)
    col = P(TP, DP)
    row = P(DP, TP)
    return jax.shard_map(
        on_device,
        mesh=fine,
        in_specs=(row, col, col, row, col, col, row, col, col, row),
        out_specs=(col, col, row),
        check_vma=False,
    )
```

```python
import jax
import jax.numpy as jnp
from jax import lax
from jax.sharding import Mesh, PartitionSpec as P

D = 8192
HID = 16384
BF16 = jnp.bfloat16
F32 = jnp.float32
DP = ("yh", "zh", "zl", "c")
TP = ("yl", "x")
NEAR = ("c", "yl", "x")


def kept(weight, mask):
    rows, cols = weight.shape
    wide = jnp.repeat(mask.astype(BF16), cols // mask.shape[1], axis=1)
    blocks = weight.reshape(mask.shape[0], rows // mask.shape[0], cols)
    return (blocks * wide[:, None, :]).reshape(rows, cols)


def swap(x, axis):
    return lax.ppermute(x, axis, [(0, 1), (1, 0)])


def exchange(pieces, axes):
    return lax.all_to_all(pieces, axes, 0, 0, tiled=True)


def together(arrays):
    return lax.optimization_barrier(arrays)


def copies(x, n):
    return jnp.broadcast_to(x[None], (n,) + x.shape)


def total(pieces, axis=0):
    return jnp.sum(pieces.astype(F32), axis=axis)


def in_order(own, other, axis):
    first = lax.axis_index(axis) == 0
    return jnp.where(first, own, other), jnp.where(first, other, own)


def dot(a, b, dims=((1,), (0,))):
    return lax.dot_general(a, b, (dims, ((), ())), preferred_element_type=F32)


def on_device(
    tokens,
    gate_weight,
    up_weight,
    down_weight,
    gate_mask,
    up_mask,
    down_mask,
    probe_gate,
    probe_up,
    probe_down,
):
    width = gate_weight.shape[1]
    feats = tokens.shape[1]

    tok0 = exchange(copies(tokens, 16), ("zl", "zh")).reshape(8, 16, feats)

    kept_gate = kept(gate_weight, gate_mask)
    kept_up = kept(up_weight, up_mask)
    kept_down = kept(down_weight, down_mask)
    stacked = jnp.concatenate([kept_gate, kept_up, probe_gate, probe_up], axis=1)
    down = jnp.concatenate([kept_down, probe_down * HID**-0.5], axis=0)
    stacked0, stacked1 = in_order(stacked, swap(stacked, "c"), "c")
    down0, down1 = in_order(down, swap(down, "c"), "c")
    tok0, stacked0, stacked1, down0, down1 = together((tok0, stacked0, stacked1, down0, down1))

    pair = jnp.stack([tok0, swap(tok0, "yh")], axis=1).reshape(-1, feats)
    partial = jnp.stack([dot(pair, stacked0).astype(BF16), dot(pair, stacked1).astype(BF16)])
    partial, pair = together((partial, pair))
    pre = exchange(partial.reshape(16, -1, 4 * width), NEAR)
    pre, pair2 = together((pre, swap(pair, "c")))
    pre = total(pre.reshape(2, 8, -1, 4 * width), 1).reshape(-1, 4 * width)

    gate = pre[:, :width]
    up = pre[:, width : 2 * width]
    tangent_gate = pre[:, 2 * width : 3 * width] * D**-0.5
    tangent_up = pre[:, 3 * width :] * D**-0.5
    sig = jax.nn.sigmoid(gate)
    act = gate * sig
    slope = sig * (1.0 + gate * (1.0 - sig))
    hid = (act * up).astype(BF16)
    tan = (slope * tangent_gate * up + act * tangent_up).astype(BF16)
    both = jnp.concatenate([tan, hid], axis=1).reshape(2, 1, 32, 2 * width)
    both = jnp.broadcast_to(both, (2, 8, 32, 2 * width)).reshape(16, 32, 2 * width)
    both = exchange(both, NEAR).reshape(2, 256, 2 * width)

    term = dot(
        jnp.concatenate([both[0], both[1]], axis=1), jnp.concatenate([down0, down1], axis=0)
    )
    term = term.astype(BF16).reshape(4, 2, 2, 16, feats)
    term = jnp.stack(in_order(term[:, :, 0], term[:, :, 1], "yh"), axis=1)
    hid0, hid1 = in_order(both[0, :, width:], both[1, :, width:], "c")
    term, hid0, hid1 = together((term.reshape(8, 32, feats), hid0, hid1))
    term = exchange(term, ("zl", "yh"))
    term, hid1 = together((term, swap(hid1, "c")))
    chunk = exchange(copies(total(term).astype(BF16), 4), "zh")
    chunk = exchange(copies(total(chunk).astype(BF16), 8), ("zl", "yh"))
    chunk = chunk.reshape(4, 2, 2, 16, feats)
    out0 = jnp.stack(in_order(chunk[:, 0], chunk[:, 1], "yh"), axis=2).reshape(-1, feats)
    out0 = together(out0)

    back = [dot(out0, d[:width], ((1,), (1,))).astype(BF16) for d in (down0, down1)]
    back = exchange(jnp.stack(back).reshape(16, 32, width), NEAR)
    back = total(back.reshape(2, 8, 32, width), 1).reshape(-1, width)
    bars = jnp.concatenate([(back * up * slope).astype(BF16), (back * act).astype(BF16)], axis=1)
    bars, out0 = together((bars, out0))
    bars = exchange(copies(bars, 8), TP).reshape(-1, 2 * width)
    out1 = swap(out0, "c")

    gathered = in_order(pair.reshape(8, 32, feats), pair2.reshape(8, 32, feats), "c")
    gathered = jnp.stack(gathered, axis=1).reshape(-1, feats)
    factor = gathered.shape[0] ** -0.5
    along = ((0,), (0,))
    grad_down = dot(
        jnp.concatenate([hid0, hid1], axis=0), jnp.concatenate([out0, out1], axis=0), along
    )
    grads = dot(gathered, bars, along)
    fisher_gate = (probe_gate.astype(F32) * grads[:, :width] * factor).astype(BF16)
    fisher_up = (probe_up.astype(F32) * grads[:, width:] * factor).astype(BF16)
    fisher_down = (probe_down.astype(F32) * grad_down * factor).astype(BF16)
    return (fisher_gate, fisher_up, fisher_down)


def solution(mesh):
    fine = Mesh(mesh.devices.reshape(2, 4, 4, 2, 2, 4), DP + TP)
    col = P(TP, DP)
    row = P(DP, TP)
    return jax.shard_map(
        on_device,
        mesh=fine,
        in_specs=(row, col, col, row, col, col, row, col, col, row),
        out_specs=(col, col, row),
        check_vma=False,
    )
```

```python
import jax
import jax.numpy as jnp
from jax import lax
from jax.experimental import pallas as pl
from jax.experimental.pallas import tpu as pltpu
from jax.sharding import Mesh, PartitionSpec as P

D = 8192
HID = 16384
TOKENS = 512
BF16 = jnp.bfloat16
F32 = jnp.float32
DP = ("yh", "zh", "zl", "c")
TP = ("yl", "x")
NEAR = ("c", "yl", "x")


def swap(x, axis):
    return lax.ppermute(x, axis, [(0, 1), (1, 0)])


def exchange(pieces, axes):
    return lax.all_to_all(pieces, axes, 0, 0, tiled=True)


def dot(a, b, dims=((1,), (0,))):
    return lax.dot_general(a, b, (dims, ((), ())), preferred_element_type=F32)


def local(kernel, outs, *args, scalars=0):
    spec = pl.BlockSpec(memory_space=pltpu.VMEM)
    small = pl.BlockSpec(memory_space=pltpu.SMEM)
    return pl.pallas_call(
        kernel,
        out_shape=[jax.ShapeDtypeStruct(shape, dtype) for shape, dtype in outs],
        in_specs=[small] * scalars + [spec] * (len(args) - scalars),
        out_specs=[spec] * len(outs),
        compiler_params=pltpu.CompilerParams(vmem_limit_bytes=32 * 2**20),
    )(*args)


def copies_kernel(x_ref, o_ref):
    for i in range(o_ref.shape[0]):
        o_ref[i] = x_ref[...]


def keep(mask_ref, w_ref, o_ref):
    for i in range(mask_ref.shape[0]):
        for j in range(mask_ref.shape[1]):
            block = (slice(i * 128, (i + 1) * 128), slice(j * 128, (j + 1) * 128))
            o_ref[block] = (w_ref[block].astype(F32) * mask_ref[i, j].astype(F32)).astype(BF16)


def kept_kernel(gmask_ref, umask_ref, gate_ref, up_ref, kgate_ref, kup_ref):
    keep(gmask_ref, gate_ref, kgate_ref)
    keep(umask_ref, up_ref, kup_ref)


def pre_kernel(
    dmask_ref,
    own_ref,
    other_ref,
    gate_ref,
    up_ref,
    pgate_ref,
    pup_ref,
    down_ref,
    pdown_ref,
    o_ref,
    down2_ref,
):
    width = gate_ref.shape[1]
    keep(dmask_ref, down_ref, down2_ref)
    down2_ref[width:, :] = pdown_ref[...]
    for half, tok_ref in enumerate((own_ref, other_ref)):
        for j, w_ref in enumerate((gate_ref, up_ref, pgate_ref, pup_ref)):
            y = dot(tok_ref[...], w_ref[...]).astype(BF16)
            for r in range(2):
                q = 16 * (2 * half + r)
                o_ref[:, q : q + 16, j * width : (j + 1) * width] = y[
                    r * 128 : (r + 1) * 128
                ].reshape(8, 16, width)


def gate_kernel(x_ref, o_ref, up_slope_ref, act_ref):
    width = act_ref.shape[1]

    def part(j):
        cols = slice(j * width, (j + 1) * width)
        acc = x_ref[0, :, cols].astype(F32)
        for i in range(1, 8):
            acc = acc + x_ref[i, :, cols].astype(F32)
        return acc

    gate = part(0)
    up = part(1)
    tangent_gate = part(2) * D**-0.5
    tangent_up = part(3) * D**-0.5
    sig = jax.nn.sigmoid(gate)
    act = gate * sig
    slope = sig * (1.0 + gate * (1.0 - sig))
    hid = (act * up).astype(BF16)
    tan = (slope * tangent_gate * up + act * tangent_up).astype(BF16)
    c = lax.axis_index("c")
    for r in range(2):
        rows = slice(r * 32, (r + 1) * 32)
        place = c if r == 0 else 1 - c
        for i in range(8):
            o_ref[place, i, :, :width] = tan[rows]
            o_ref[place, i, :, width:] = hid[rows]
    up_slope_ref[...] = up * slope
    act_ref[...] = act


def term_kernel(x_ref, down_ref, down2_ref, o_ref, hid_ref, hid2_ref):
    width = hid_ref.shape[1]
    c = lax.axis_index("c")
    yh = lax.axis_index("yh")

    def rows(src):
        parts = [x_ref[src, :, 16 * r : 16 * r + 16, :].reshape(128, 2 * width) for r in range(2)]
        return jnp.concatenate(parts, axis=0)

    own = rows(c)
    other = rows(1 - c)
    hid_ref[...] = own[:, width:]
    hid2_ref[...] = other[:, width:]
    for j in range(4):
        cols = slice(j * 256, (j + 1) * 256)
        y = dot(own[:, width:], down_ref[width:, cols]) + dot(other[:, width:], down2_ref[width:, cols])
        y = y * HID**-0.5
        y = y + dot(own[:, :width], down_ref[:width, cols])
        y = y + dot(other[:, :width], down2_ref[:width, cols])
        y = y.astype(BF16)
        for r in range(2):
            place = yh if r == 0 else 1 - yh
            o_ref[:, place, :, cols] = y[r * 128 : (r + 1) * 128].reshape(4, 32, 256)


def spread_kernel(x_ref, o_ref):
    acc = x_ref[0].astype(F32)
    for i in range(1, x_ref.shape[0]):
        acc = acc + x_ref[i].astype(F32)
    acc = acc.astype(BF16)
    for i in range(o_ref.shape[0]):
        o_ref[i] = acc


def back_kernel(x_ref, down_ref, down2_ref, o_ref, out_ref):
    width = o_ref.shape[3]
    c = lax.axis_index("c")
    yh = lax.axis_index("yh")
    for r in range(2):
        place = yh if r == 0 else 1 - yh
        out_ref[r * 128 : (r + 1) * 128, :] = x_ref[:, place].reshape(128, x_ref.shape[3])
    for w_ref, place in ((down_ref, c), (down2_ref, 1 - c)):
        y = dot(out_ref[...], w_ref[:width, :], ((1,), (1,))).astype(BF16)
        for r in range(2):
            o_ref[place, :, 16 * r : 16 * r + 16, :] = y[r * 128 : (r + 1) * 128].reshape(
                8, 16, width
            )


def bars_kernel(x_ref, up_slope_ref, act_ref, o_ref):
    width = act_ref.shape[1]
    c = lax.axis_index("c")
    for r in range(2):
        place = c if r == 0 else 1 - c
        rows = slice(r * 32, (r + 1) * 32)
        back = x_ref[place, 0].astype(F32)
        for i in range(1, 8):
            back = back + x_ref[place, i].astype(F32)
        gate_bar = (back * up_slope_ref[rows]).astype(BF16)
        up_bar = (back * act_ref[rows]).astype(BF16)
        for i in range(8):
            o_ref[i, rows, :width] = gate_bar
            o_ref[i, rows, width:] = up_bar


def fisher_kernel(own_ref, other_ref, bars_ref, pgate_ref, pup_ref, gate_ref, up_ref):
    width = gate_ref.shape[1]
    factor = TOKENS**-0.5
    bars = [bars_ref[:, 16 * q : 16 * q + 16, :].reshape(128, 2 * width) for q in range(4)]
    y = dot(own_ref[...], jnp.concatenate(bars[:2], axis=0), ((0,), (0,)))
    y = y + dot(other_ref[...], jnp.concatenate(bars[2:], axis=0), ((0,), (0,)))
    gate_ref[...] = (pgate_ref[...].astype(F32) * y[:, :width] * factor).astype(BF16)
    up_ref[...] = (pup_ref[...].astype(F32) * y[:, width:] * factor).astype(BF16)


def fisher(own, other, bars, probe_gate, probe_up):
    rows, width = probe_gate.shape
    block = 256
    weight = pl.BlockSpec((block, width), lambda i: (i, 0))
    return pl.pallas_call(
        fisher_kernel,
        grid=(rows // block,),
        out_shape=[jax.ShapeDtypeStruct((rows, width), BF16)] * 2,
        in_specs=[
            pl.BlockSpec((own.shape[0], block), lambda i: (0, i)),
            pl.BlockSpec((own.shape[0], block), lambda i: (0, i)),
            pl.BlockSpec(bars.shape, lambda i: (0, 0, 0)),
            weight,
            weight,
        ],
        out_specs=[weight, weight],
        compiler_params=pltpu.CompilerParams(vmem_limit_bytes=32 * 2**20),
    )(own, other, bars, probe_gate, probe_up)


def on_device(
    tokens,
    gate_weight,
    up_weight,
    down_weight,
    gate_mask,
    up_mask,
    down_mask,
    probe_gate,
    probe_up,
    probe_down,
):
    width = gate_weight.shape[1]
    feats = tokens.shape[1]

    (mine,) = local(copies_kernel, [((16, 8, feats), BF16)], tokens)
    tok0 = exchange(mine, ("zl", "zh")).reshape(128, feats)
    kept_gate, kept_up = local(
        kept_kernel,
        [(gate_weight.shape, BF16), (up_weight.shape, BF16)],
        gate_mask,
        up_mask,
        gate_weight,
        up_weight,
        scalars=2,
    )
    pair = jnp.concatenate([tok0, swap(tok0, "yh")], axis=0)
    pair2 = swap(pair, "c")
    partial, down = local(
        pre_kernel,
        [((8, 64, 4 * width), BF16), ((2 * width, feats), BF16)],
        down_mask,
        pair,
        pair2,
        kept_gate,
        kept_up,
        probe_gate,
        probe_up,
        down_weight,
        probe_down,
        scalars=1,
    )
    pre = exchange(partial, TP)
    down2 = swap(down, "c")
    send, up_slope, act = local(
        gate_kernel,
        [((2, 8, 32, 2 * width), BF16), ((64, width), F32), ((64, width), F32)],
        pre,
    )
    both = exchange(send.reshape(16, 32, 2 * width), NEAR).reshape(2, 8, 32, 2 * width)
    term, hid, hid2 = local(
        term_kernel,
        [((4, 2, 32, feats), BF16), ((256, width), BF16), ((256, width), BF16)],
        both,
        down,
        down2,
    )
    term = exchange(term.reshape(8, 32, feats), ("zl", "yh"))
    (chunk,) = local(spread_kernel, [((4, 32, feats), BF16)], term)
    chunk = exchange(chunk, "zh")
    (chunk,) = local(spread_kernel, [((8, 32, feats), BF16)], chunk)
    chunk = exchange(chunk, ("zl", "yh")).reshape(4, 2, 32, feats)
    back, out = local(
        back_kernel, [((2, 8, 32, width), BF16), ((256, feats), BF16)], chunk, down, down2
    )
    back = exchange(back.reshape(16, 32, width), NEAR).reshape(2, 8, 32, width)
    (bars,) = local(bars_kernel, [((8, 64, 2 * width), BF16)], back, up_slope, act)
    bars = exchange(bars, TP)

    grad_down = dot(
        jnp.concatenate([hid, swap(hid2, "c")], axis=0),
        jnp.concatenate([out, swap(out, "c")], axis=0),
        ((0,), (0,)),
    )
    fisher_down = (probe_down.astype(F32) * grad_down * TOKENS**-0.5).astype(BF16)
    fisher_gate, fisher_up = fisher(pair, pair2, bars, probe_gate, probe_up)
    return (fisher_gate, fisher_up, fisher_down)


def solution(mesh):
    fine = Mesh(mesh.devices.reshape(2, 4, 4, 2, 2, 4), DP + TP)
    col = P(TP, DP)
    row = P(DP, TP)
    return jax.shard_map(
        on_device,
        mesh=fine,
        in_specs=(row, col, col, row, col, col, row, col, col, row),
        out_specs=(col, col, row),
        check_vma=False,
    )
```

```python
import jax
import jax.numpy as jnp
from jax import lax
from jax.experimental import pallas as pl
from jax.experimental.pallas import tpu as pltpu
from jax.sharding import Mesh, PartitionSpec as P

D = 8192
HID = 16384
TOKENS = 512
BF16 = jnp.bfloat16
F32 = jnp.float32
DP = ("yh", "zh", "zl", "c")
TP = ("yl", "x")
NEAR = ("yh", "c", "yl", "x")


def swap(x, axis):
    return lax.ppermute(x, axis, [(0, 1), (1, 0)])


def step_y(x, way):
    return lax.ppermute(x, ("yh", "yl"), [(i, (i + way) % 4) for i in range(4)])


def exchange(pieces, axes):
    return lax.all_to_all(pieces, axes, 0, 0, tiled=True)


def dot(a, b, dims=((1,), (0,))):
    return lax.dot_general(a, b, (dims, ((), ())), preferred_element_type=F32)


def local(kernel, outs, *args, scalars=0, after=0):
    spec = pl.BlockSpec(memory_space=pltpu.VMEM)
    small = pl.BlockSpec(memory_space=pltpu.SMEM)
    unread = pl.BlockSpec(memory_space=pl.ANY)
    return pl.pallas_call(
        kernel,
        out_shape=[jax.ShapeDtypeStruct(shape, dtype) for shape, dtype in outs],
        in_specs=[small] * scalars + [spec] * (len(args) - scalars - after) + [unread] * after,
        out_specs=[spec] * len(outs),
        compiler_params=pltpu.CompilerParams(vmem_limit_bytes=32 * 2**20),
    )(*args)


def relatives():
    c = lax.axis_index("c")
    yh = lax.axis_index("yh")
    for dy, y in enumerate((yh, 1 - yh)):
        for dc, core in enumerate((c, 1 - c)):
            yield dy, dc, 2 * y + core


def copies_kernel(x_ref, o_ref):
    for i in range(o_ref.shape[0]):
        o_ref[i] = x_ref[...]


def keep(mask_ref, w_ref, o_ref):
    for i in range(mask_ref.shape[0]):
        for j in range(mask_ref.shape[1]):
            block = (slice(i * 128, (i + 1) * 128), slice(j * 128, (j + 1) * 128))
            o_ref[block] = (w_ref[block].astype(F32) * mask_ref[i, j].astype(F32)).astype(BF16)


def keep_kernel(mask_ref, w_ref, o_ref):
    keep(mask_ref, w_ref, o_ref)


def stack_kernel(gmask_ref, umask_ref, gate_ref, up_ref, pgate_ref, pup_ref, o_ref):
    width = gate_ref.shape[1]
    keep(gmask_ref, gate_ref, o_ref.at[:, :width])
    keep(umask_ref, up_ref, o_ref.at[:, width : 2 * width])
    o_ref[:, 2 * width : 3 * width] = pgate_ref[...]
    o_ref[:, 3 * width :] = pup_ref[...]


def pair_kernel(a_ref, b_ref, *refs):
    o_ref = refs[-1]
    rows = a_ref.shape[0]
    o_ref[:rows] = a_ref[...]
    o_ref[rows:] = b_ref[...]


def pre_kernel(own_ref, other_ref, w_ref, o_ref):
    width = w_ref.shape[1] // 4
    for half, tok_ref in enumerate((own_ref, other_ref)):
        for j in range(4):
            cols = slice(j * width, (j + 1) * width)
            y = dot(tok_ref[...], w_ref[:, cols]).astype(BF16)
            for r in range(2):
                q = 16 * (2 * half + r)
                o_ref[:, q : q + 16, cols] = y[r * 128 : (r + 1) * 128].reshape(8, 16, width)


def pack_kernel(kept_ref, probe_ref, kept2_ref, probe2_ref, after_ref, o_ref):
    width = kept_ref.shape[0]
    scale = HID**-0.5
    o_ref[:width] = kept_ref[...]
    o_ref[width : 2 * width] = (probe_ref[...].astype(F32) * scale).astype(BF16)
    o_ref[2 * width : 3 * width] = kept2_ref[...]
    o_ref[3 * width :] = (probe2_ref[...].astype(F32) * scale).astype(BF16)


def gate_kernel(x_ref, o_ref, up_slope_ref, act_ref):
    width = act_ref.shape[1]

    def part(j):
        cols = slice(j * width, (j + 1) * width)
        acc = x_ref[0, :, cols].astype(F32)
        for i in range(1, 8):
            acc = acc + x_ref[i, :, cols].astype(F32)
        return acc

    gate = part(0)
    up = part(1)
    tangent_gate = part(2) * D**-0.5
    tangent_up = part(3) * D**-0.5
    sig = jax.nn.sigmoid(gate)
    act = gate * sig
    slope = sig * (1.0 + gate * (1.0 - sig))
    hid = (act * up).astype(BF16)
    tan = (slope * tangent_gate * up + act * tangent_up).astype(BF16)
    for dy, dc, place in relatives():
        q = 16 * (2 * dc + dy)
        for i in range(8):
            o_ref[place, i, :, :width] = tan[q : q + 16]
            o_ref[place, i, :, width:] = hid[q : q + 16]
    up_slope_ref[...] = up * slope
    act_ref[...] = act


def term_kernel(x_ref, down_ref, down2_ref, o_ref, hid_ref, hid2_ref):
    width = hid_ref.shape[1]
    rows = [[], []]
    for dy, dc, place in relatives():
        part = x_ref[place].reshape(128, 2 * width)
        rows[dc].append(part)
        (hid_ref, hid2_ref)[dc][dy * 128 : (dy + 1) * 128, :] = part[:, width:]
    own = jnp.concatenate(rows[0], axis=1)
    other = jnp.concatenate(rows[1], axis=1)
    for j in range(4):
        cols = slice(j * 256, (j + 1) * 256)
        y = dot(own, down_ref[:, cols]) + dot(other, down2_ref[:, cols])
        o_ref[:, :, cols] = y.astype(BF16).reshape(4, 32, 256)


def spread_kernel(x_ref, *refs):
    o_ref = refs[-1]
    acc = x_ref[0].astype(F32)
    for i in range(1, x_ref.shape[0]):
        acc = acc + x_ref[i].astype(F32)
    acc = acc.astype(BF16)
    for i in range(o_ref.shape[0]):
        o_ref[i] = acc


def back_kernel(x_ref, down_ref, down2_ref, after_ref, o_ref):
    width = o_ref.shape[3]
    for dy, dc, place in relatives():
        w_ref = (down_ref, down2_ref)[dc]
        y = dot(x_ref[...], w_ref[2 * dy * width : (2 * dy + 1) * width, :], ((1,), (1,)))
        o_ref[place] = y.astype(BF16).reshape(8, 16, width)


def later_kernel(x_ref, after_ref, o_ref):
    o_ref[...] = x_ref[...]


def bars_kernel(x_ref, up_slope_ref, act_ref, o_ref):
    width = act_ref.shape[1]
    for dy, dc, place in relatives():
        q = 16 * (2 * dc + dy)
        rows = slice(q, q + 16)
        back = x_ref[place, 0].astype(F32)
        for i in range(1, 8):
            back = back + x_ref[place, i].astype(F32)
        gate_bar = (back * up_slope_ref[rows]).astype(BF16)
        up_bar = (back * act_ref[rows]).astype(BF16)
        for i in range(8):
            o_ref[i, rows, :width] = gate_bar
            o_ref[i, rows, width:] = up_bar


def fisher_kernel(
    own_ref, other_ref, bars_ref, pgate_ref, pup_ref, after_ref, gate_ref, up_ref
):
    width = gate_ref.shape[1]
    factor = TOKENS**-0.5
    bars = [bars_ref[:, 16 * q : 16 * q + 16, :].reshape(128, 2 * width) for q in range(4)]
    y = dot(own_ref[...], jnp.concatenate(bars[:2], axis=0), ((0,), (0,)))
    y = y + dot(other_ref[...], jnp.concatenate(bars[2:], axis=0), ((0,), (0,)))
    gate_ref[...] = (pgate_ref[...].astype(F32) * y[:, :width] * factor).astype(BF16)
    up_ref[...] = (pup_ref[...].astype(F32) * y[:, width:] * factor).astype(BF16)


def fisher(own, other, bars, probe_gate, probe_up, after):
    rows, width = probe_gate.shape
    block = 256
    weight = pl.BlockSpec((block, width), lambda i: (i, 0))
    return pl.pallas_call(
        fisher_kernel,
        grid=(rows // block,),
        out_shape=[jax.ShapeDtypeStruct((rows, width), BF16)] * 2,
        in_specs=[
            pl.BlockSpec((own.shape[0], block), lambda i: (0, i)),
            pl.BlockSpec((own.shape[0], block), lambda i: (0, i)),
            pl.BlockSpec(bars.shape, lambda i: (0, 0, 0)),
            weight,
            weight,
            pl.BlockSpec(memory_space=pl.ANY),
        ],
        out_specs=[weight, weight],
        compiler_params=pltpu.CompilerParams(vmem_limit_bytes=32 * 2**20),
    )(own, other, bars, probe_gate, probe_up, after)


def on_device(
    tokens,
    gate_weight,
    up_weight,
    down_weight,
    gate_mask,
    up_mask,
    down_mask,
    probe_gate,
    probe_up,
    probe_down,
):
    width = gate_weight.shape[1]
    feats = tokens.shape[1]

    (kept_down,) = local(
        keep_kernel, [(down_weight.shape, BF16)], down_mask, down_weight, scalars=1
    )
    (mine,) = local(copies_kernel, [((16, 8, feats), BF16)], tokens)
    tok0 = exchange(mine, ("zl", "zh")).reshape(128, feats)
    kept_y = swap(kept_down, "yh")
    probe_y = step_y(probe_down, -1)
    (stacked,) = local(
        stack_kernel,
        [((feats, 4 * width), BF16)],
        gate_mask,
        up_mask,
        gate_weight,
        up_weight,
        probe_gate,
        probe_up,
        scalars=2,
    )
    tok1 = swap(tok0, "yh")
    (pair,) = local(
        pair_kernel, [((256, feats), BF16)], tok0, tok1, stacked, kept_y, probe_y, after=3
    )
    probe_y = step_y(probe_y, -1)
    pair2 = swap(pair, "c")
    (partial,) = local(pre_kernel, [((8, 64, 4 * width), BF16)], pair, pair2, stacked)
    pre = exchange(partial, TP)
    (down,) = local(
        pack_kernel,
        [((4 * width, feats), BF16)],
        kept_down,
        probe_down,
        kept_y,
        probe_y,
        partial,
        after=1,
    )
    down2 = swap(down, "c")
    send, up_slope, act = local(
        gate_kernel,
        [((4, 8, 16, 2 * width), BF16), ((64, width), F32), ((64, width), F32)],
        pre,
    )
    both = exchange(send.reshape(32, 16, 2 * width), NEAR).reshape(4, 8, 16, 2 * width)
    term, hid, hid2 = local(
        term_kernel,
        [((4, 32, feats), BF16), ((256, width), BF16), ((256, width), BF16)],
        both,
        down,
        down2,
    )
    term = exchange(term, "zl")
    hid2 = swap(hid2, "c")
    (chunk,) = local(spread_kernel, [((4, 32, feats), BF16)], term, hid2, after=1)
    far = swap(jnp.concatenate([hid[128:], hid2[128:]], axis=0), "yh")
    hidden = jnp.concatenate([hid[:128], far[:128], hid2[:128], far[128:]], axis=0)
    chunk = exchange(chunk, "zh")
    (chunk,) = local(spread_kernel, [((4, 32, feats), BF16)], chunk)
    out = exchange(chunk, "zl").reshape(128, feats)
    (back,) = local(
        back_kernel, [((4, 8, 16, width), BF16)], out, down, down2, hidden, after=1
    )
    back_sum = exchange(back.reshape(32, 16, width), NEAR).reshape(4, 8, 16, width)

    (late,) = local(later_kernel, [((128, feats), BF16)], out, back, after=1)
    outs = jnp.concatenate([late, swap(late, "yh")], axis=0)

    (bars,) = local(bars_kernel, [((8, 64, 2 * width), BF16)], back_sum, up_slope, act)
    bars = exchange(bars, TP)
    outs = jnp.concatenate([outs, swap(outs, "c")], axis=0)
    grad_down = dot(hidden, outs, ((0,), (0,)))
    fisher_down = (probe_down.astype(F32) * grad_down * TOKENS**-0.5).astype(BF16)
    fisher_gate, fisher_up = fisher(pair, pair2, bars, probe_gate, probe_up, fisher_down)
    return (fisher_gate, fisher_up, fisher_down)


def solution(mesh):
    fine = Mesh(mesh.devices.reshape(2, 4, 4, 2, 2, 4), DP + TP)
    col = P(TP, DP)
    row = P(DP, TP)
    return jax.shard_map(
        on_device,
        mesh=fine,
        in_specs=(row, col, col, row, col, col, row, col, col, row),
        out_specs=(col, col, row),
        check_vma=False,
    )
```

```python
import jax
import jax.numpy as jnp
from jax import lax
from jax.experimental import pallas as pl
from jax.experimental.pallas import tpu as pltpu
from jax.sharding import Mesh, PartitionSpec as P

D = 8192
HID = 16384
TOKENS = 512
BF16 = jnp.bfloat16
F32 = jnp.float32
DP = ("yh", "zh", "zl", "c")
TP = ("yl", "x")
NEAR = ("c", "yl", "x")


def swap(x, axis):
    return lax.ppermute(x, axis, [(0, 1), (1, 0)])


def exchange(pieces, axes):
    return lax.all_to_all(pieces, axes, 0, 0, tiled=True)


def dot(a, b, dims=((1,), (0,))):
    return lax.dot_general(a, b, (dims, ((), ())), preferred_element_type=F32)


def local(kernel, outs, *args, scalars=0, after=0):
    spec = pl.BlockSpec(memory_space=pltpu.VMEM)
    small = pl.BlockSpec(memory_space=pltpu.SMEM)
    unread = pl.BlockSpec(memory_space=pl.ANY)
    return pl.pallas_call(
        kernel,
        out_shape=[jax.ShapeDtypeStruct(shape, dtype) for shape, dtype in outs],
        in_specs=[small] * scalars + [spec] * (len(args) - scalars - after) + [unread] * after,
        out_specs=[spec] * len(outs),
        compiler_params=pltpu.CompilerParams(vmem_limit_bytes=16 * 2**20),
    )(*args)


def copies_kernel(x_ref, o_ref):
    for i in range(o_ref.shape[0]):
        o_ref[i] = x_ref[...]


def keep(mask_ref, w_ref, o_ref):
    for i in range(mask_ref.shape[0]):
        for j in range(mask_ref.shape[1]):
            block = (slice(i * 128, (i + 1) * 128), slice(j * 128, (j + 1) * 128))
            o_ref[block] = (w_ref[block].astype(F32) * mask_ref[i, j].astype(F32)).astype(BF16)


def stack_kernel(gmask_ref, umask_ref, gate_ref, up_ref, pgate_ref, pup_ref, o_ref):
    width = gate_ref.shape[1]
    keep(gmask_ref, gate_ref, o_ref.at[:, :width])
    keep(umask_ref, up_ref, o_ref.at[:, width : 2 * width])
    o_ref[:, 2 * width : 3 * width] = pgate_ref[...]
    o_ref[:, 3 * width :] = pup_ref[...]


def pair_kernel(a_ref, b_ref, *refs):
    o_ref = refs[-1]
    rows = a_ref.shape[0]
    o_ref[:rows] = a_ref[...]
    o_ref[rows:] = b_ref[...]


def pre_kernel(own_ref, other_ref, w_ref, o_ref):
    width = w_ref.shape[1] // 4
    for half, tok_ref in enumerate((own_ref, other_ref)):
        for j in range(4):
            cols = slice(j * width, (j + 1) * width)
            y = dot(tok_ref[...], w_ref[:, cols]).astype(BF16)
            for r in range(2):
                q = 16 * (2 * half + r)
                o_ref[:, q : q + 16, cols] = y[r * 128 : (r + 1) * 128].reshape(8, 16, width)


def down_kernel(mask_ref, down_ref, probe_ref, o_ref):
    width = down_ref.shape[0]
    keep(mask_ref, down_ref, o_ref.at[:width, :])
    o_ref[width:, :] = probe_ref[...]


def gate_kernel(x_ref, o_ref, up_slope_ref, act_ref):
    width = act_ref.shape[1]

    def part(j):
        cols = slice(j * width, (j + 1) * width)
        acc = x_ref[0, :, cols].astype(F32)
        for i in range(1, 8):
            acc = acc + x_ref[i, :, cols].astype(F32)
        return acc

    gate = part(0)
    up = part(1)
    tangent_gate = part(2) * D**-0.5
    tangent_up = part(3) * D**-0.5
    sig = jax.nn.sigmoid(gate)
    act = gate * sig
    slope = sig * (1.0 + gate * (1.0 - sig))
    hid = (act * up).astype(BF16)
    tan = (slope * tangent_gate * up + act * tangent_up).astype(BF16)
    c = lax.axis_index("c")
    for r in range(2):
        rows = slice(r * 32, (r + 1) * 32)
        place = c if r == 0 else 1 - c
        for i in range(8):
            o_ref[place, i, :, :width] = tan[rows]
            o_ref[place, i, :, width:] = hid[rows]
    up_slope_ref[...] = up * slope
    act_ref[...] = act


def term_kernel(x_ref, down_ref, down2_ref, o_ref, hid_ref, hid2_ref):
    width = hid_ref.shape[1]
    c = lax.axis_index("c")
    yh = lax.axis_index("yh")

    def rows(src):
        parts = [x_ref[src, :, 16 * r : 16 * r + 16, :].reshape(128, 2 * width) for r in range(2)]
        return jnp.concatenate(parts, axis=0)

    own = rows(c)
    other = rows(1 - c)
    hid_ref[...] = own[:, width:]
    hid2_ref[...] = other[:, width:]
    for j in range(4):
        cols = slice(j * 256, (j + 1) * 256)
        y = dot(own[:, width:], down_ref[width:, cols]) + dot(other[:, width:], down2_ref[width:, cols])
        y = y * HID**-0.5
        y = y + dot(own[:, :width], down_ref[:width, cols])
        y = y + dot(other[:, :width], down2_ref[:width, cols])
        y = y.astype(BF16)
        for r in range(2):
            place = yh if r == 0 else 1 - yh
            o_ref[:, place, :, cols] = y[r * 128 : (r + 1) * 128].reshape(4, 32, 256)


def spread_kernel(x_ref, *refs):
    o_ref = refs[-1]
    acc = x_ref[0].astype(F32)
    for i in range(1, x_ref.shape[0]):
        acc = acc + x_ref[i].astype(F32)
    acc = acc.astype(BF16)
    for i in range(o_ref.shape[0]):
        o_ref[i] = acc


def back_kernel(x_ref, down_ref, down2_ref, o_ref, out_ref):
    width = o_ref.shape[3]
    c = lax.axis_index("c")
    yh = lax.axis_index("yh")
    for r in range(2):
        place = yh if r == 0 else 1 - yh
        out_ref[r * 128 : (r + 1) * 128, :] = x_ref[:, place].reshape(128, x_ref.shape[3])
    for w_ref, place in ((down_ref, c), (down2_ref, 1 - c)):
        y = dot(out_ref[...], w_ref[:width, :], ((1,), (1,))).astype(BF16)
        for r in range(2):
            o_ref[place, :, 16 * r : 16 * r + 16, :] = y[r * 128 : (r + 1) * 128].reshape(
                8, 16, width
            )


def later_kernel(x_ref, after_ref, o_ref):
    o_ref[...] = x_ref[...]


def turn_kernel(a_ref, b_ref, after_ref, o_ref):
    rows = a_ref.shape[0]
    o_ref[:, :rows] = a_ref[...].T
    o_ref[:, rows:] = b_ref[...].T


def bars_kernel(x_ref, up_slope_ref, act_ref, o_ref):
    width = act_ref.shape[1]
    c = lax.axis_index("c")
    for r in range(2):
        place = c if r == 0 else 1 - c
        rows = slice(r * 32, (r + 1) * 32)
        back = x_ref[place, 0].astype(F32)
        for i in range(1, 8):
            back = back + x_ref[place, i].astype(F32)
        gate_bar = (back * up_slope_ref[rows]).astype(BF16)
        up_bar = (back * act_ref[rows]).astype(BF16)
        for i in range(8):
            o_ref[i, rows, :width] = gate_bar
            o_ref[i, rows, width:] = up_bar


def fisher_kernel(tok_ref, bars_ref, pgate_ref, pup_ref, after_ref, gate_ref, up_ref):
    width = gate_ref.shape[1]
    factor = TOKENS**-0.5
    bars = [bars_ref[:, 16 * q : 16 * q + 16, :].reshape(128, 2 * width) for q in range(4)]
    y = dot(tok_ref[...], jnp.concatenate(bars, axis=0))
    gate_ref[...] = (pgate_ref[...].astype(F32) * y[:, :width] * factor).astype(BF16)
    up_ref[...] = (pup_ref[...].astype(F32) * y[:, width:] * factor).astype(BF16)


def fisher(tok, bars, probe_gate, probe_up, after):
    rows, width = probe_gate.shape
    block = 256
    weight = pl.BlockSpec((block, width), lambda i: (i, 0))
    return pl.pallas_call(
        fisher_kernel,
        grid=(rows // block,),
        out_shape=[jax.ShapeDtypeStruct((rows, width), BF16)] * 2,
        in_specs=[
            pl.BlockSpec((block, tok.shape[1]), lambda i: (i, 0)),
            pl.BlockSpec(bars.shape, lambda i: (0, 0, 0)),
            weight,
            weight,
            pl.BlockSpec(memory_space=pl.ANY),
        ],
        out_specs=[weight, weight],
        compiler_params=pltpu.CompilerParams(vmem_limit_bytes=16 * 2**20),
    )(tok, bars, probe_gate, probe_up, after)


def on_device(
    tokens,
    gate_weight,
    up_weight,
    down_weight,
    gate_mask,
    up_mask,
    down_mask,
    probe_gate,
    probe_up,
    probe_down,
):
    width = gate_weight.shape[1]
    feats = tokens.shape[1]

    (mine,) = local(copies_kernel, [((16, 8, feats), BF16)], tokens)
    tok0 = exchange(mine, ("zl", "zh")).reshape(128, feats)
    (stacked,) = local(
        stack_kernel,
        [((feats, 4 * width), BF16)],
        gate_mask,
        up_mask,
        gate_weight,
        up_weight,
        probe_gate,
        probe_up,
        scalars=2,
    )
    (down,) = local(
        down_kernel, [((2 * width, feats), BF16)], down_mask, down_weight, probe_down, scalars=1
    )
    down2 = swap(down, "c")
    tok1 = swap(tok0, "yh")
    (pair,) = local(pair_kernel, [((256, feats), BF16)], tok0, tok1, stacked, down2, after=2)
    pair2 = swap(pair, "c")
    (partial,) = local(pre_kernel, [((8, 64, 4 * width), BF16)], pair, pair2, stacked)
    pre = exchange(partial, TP)
    send, up_slope, act = local(
        gate_kernel,
        [((2, 8, 32, 2 * width), BF16), ((64, width), F32), ((64, width), F32)],
        pre,
    )
    both = exchange(send.reshape(16, 32, 2 * width), NEAR).reshape(2, 8, 32, 2 * width)
    term, hid, hid2 = local(
        term_kernel,
        [((4, 2, 32, feats), BF16), ((256, width), BF16), ((256, width), BF16)],
        both,
        down,
        down2,
    )
    term = exchange(term.reshape(8, 32, feats), ("zl", "yh"))
    hid2 = swap(hid2, "c")
    (chunk,) = local(spread_kernel, [((4, 32, feats), BF16)], term, hid2, after=1)
    (tok_t,) = local(turn_kernel, [((feats, TOKENS), BF16)], pair, pair2, chunk, after=1)
    chunk = exchange(chunk, "zh")
    (chunk,) = local(spread_kernel, [((8, 32, feats), BF16)], chunk, tok_t, after=1)
    chunk = exchange(chunk, ("zl", "yh")).reshape(4, 2, 32, feats)
    back, out = local(
        back_kernel, [((2, 8, 32, width), BF16), ((256, feats), BF16)], chunk, down, down2
    )
    back = exchange(back.reshape(16, 32, width), NEAR).reshape(2, 8, 32, width)
    (bars,) = local(bars_kernel, [((8, 64, 2 * width), BF16)], back, up_slope, act)
    (late,) = local(later_kernel, [(out.shape, BF16)], out, bars, after=1)
    bars = exchange(bars, TP)

    grad_down = dot(
        jnp.concatenate([hid, hid2], axis=0),
        jnp.concatenate([late, swap(late, "c")], axis=0),
        ((0,), (0,)),
    )
    fisher_down = (probe_down.astype(F32) * grad_down * TOKENS**-0.5).astype(BF16)
    fisher_gate, fisher_up = fisher(tok_t, bars, probe_gate, probe_up, fisher_down)
    return (fisher_gate, fisher_up, fisher_down)


def solution(mesh):
    fine = Mesh(mesh.devices.reshape(2, 4, 4, 2, 2, 4), DP + TP)
    col = P(TP, DP)
    row = P(DP, TP)
    return jax.shard_map(
        on_device,
        mesh=fine,
        in_specs=(row, col, col, row, col, col, row, col, col, row),
        out_specs=(col, col, row),
        check_vma=False,
    )
```

```python
import jax
import jax.numpy as jnp
from jax import lax
from jax.experimental import pallas as pl
from jax.experimental.pallas import tpu as pltpu
from jax.sharding import Mesh, PartitionSpec as P

D = 8192
HID = 16384
TOKENS = 512
BF16 = jnp.bfloat16
F32 = jnp.float32
DP = ("yh", "zh", "zl", "c")
TP = ("yl", "x")
NEAR = ("c", "yl", "x")


def swap(x, axis):
    return lax.ppermute(x, axis, [(0, 1), (1, 0)])


def exchange(pieces, axes):
    return lax.all_to_all(pieces, axes, 0, 0, tiled=True)


def dot(a, b, dims=((1,), (0,))):
    return lax.dot_general(a, b, (dims, ((), ())), preferred_element_type=F32)


def local(kernel, outs, *args, scalars=0, after=0):
    spec = pl.BlockSpec(memory_space=pltpu.VMEM)
    small = pl.BlockSpec(memory_space=pltpu.SMEM)
    unread = pl.BlockSpec(memory_space=pl.ANY)
    return pl.pallas_call(
        kernel,
        out_shape=[jax.ShapeDtypeStruct(shape, dtype) for shape, dtype in outs],
        in_specs=[small] * scalars + [spec] * (len(args) - scalars - after) + [unread] * after,
        out_specs=[spec] * len(outs),
        compiler_params=pltpu.CompilerParams(vmem_limit_bytes=16 * 2**20),
    )(*args)


def copies_kernel(x_ref, o_ref):
    for i in range(o_ref.shape[0]):
        o_ref[i] = x_ref[...]


def keep(mask_ref, w_ref, o_ref):
    for i in range(mask_ref.shape[0]):
        for j in range(mask_ref.shape[1]):
            block = (slice(i * 128, (i + 1) * 128), slice(j * 128, (j + 1) * 128))
            o_ref[block] = (w_ref[block].astype(F32) * mask_ref[i, j].astype(F32)).astype(BF16)


def stack_kernel(gmask_ref, umask_ref, gate_ref, up_ref, pgate_ref, pup_ref, o_ref):
    width = gate_ref.shape[1]
    keep(gmask_ref, gate_ref, o_ref.at[:, :width])
    keep(umask_ref, up_ref, o_ref.at[:, width : 2 * width])
    o_ref[:, 2 * width : 3 * width] = pgate_ref[...]
    o_ref[:, 3 * width :] = pup_ref[...]


def pre_kernel(own_ref, other_ref, w_ref, *refs):
    o_ref = refs[-1]
    width = w_ref.shape[1] // 4
    for half, tok_ref in enumerate((own_ref, other_ref)):
        for j in range(4):
            cols = slice(j * width, (j + 1) * width)
            y = dot(tok_ref[...], w_ref[:, cols]).astype(BF16)
            for r in range(2):
                q = 16 * (2 * half + r)
                o_ref[:, q : q + 16, cols] = y[r * 128 : (r + 1) * 128].reshape(8, 16, width)


def down_kernel(mask_ref, down_ref, probe_ref, o_ref):
    width = down_ref.shape[0]
    keep(mask_ref, down_ref, o_ref.at[:width, :])
    o_ref[width:, :] = probe_ref[...]


def gate_kernel(x_ref, o_ref, up_slope_ref, act_ref):
    width = act_ref.shape[1]

    def part(j):
        cols = slice(j * width, (j + 1) * width)
        acc = x_ref[0, :, cols].astype(F32)
        for i in range(1, 8):
            acc = acc + x_ref[i, :, cols].astype(F32)
        return acc

    gate = part(0)
    up = part(1)
    tangent_gate = part(2) * D**-0.5
    tangent_up = part(3) * D**-0.5
    sig = jax.nn.sigmoid(gate)
    act = gate * sig
    slope = sig * (1.0 + gate * (1.0 - sig))
    hid = (act * up).astype(BF16)
    tan = (slope * tangent_gate * up + act * tangent_up).astype(BF16)
    c = lax.axis_index("c")
    for r in range(2):
        rows = slice(r * 32, (r + 1) * 32)
        place = c if r == 0 else 1 - c
        for i in range(8):
            o_ref[place, i, :, :width] = tan[rows]
            o_ref[place, i, :, width:] = hid[rows]
    up_slope_ref[...] = up * slope
    act_ref[...] = act


def term_kernel(x_ref, down_ref, down2_ref, o_ref, hid_ref, hid2_ref):
    width = hid_ref.shape[1]
    c = lax.axis_index("c")
    yh = lax.axis_index("yh")

    def rows(src):
        parts = [x_ref[src, :, 16 * r : 16 * r + 16, :].reshape(128, 2 * width) for r in range(2)]
        return jnp.concatenate(parts, axis=0)

    own = rows(c)
    other = rows(1 - c)
    hid_ref[...] = own[:, width:]
    hid2_ref[...] = other[:, width:]
    for j in range(4):
        cols = slice(j * 256, (j + 1) * 256)
        y = dot(own[:, width:], down_ref[width:, cols]) + dot(other[:, width:], down2_ref[width:, cols])
        y = y * HID**-0.5
        y = y + dot(own[:, :width], down_ref[:width, cols])
        y = y + dot(other[:, :width], down2_ref[:width, cols])
        y = y.astype(BF16)
        for r in range(2):
            place = yh if r == 0 else 1 - yh
            o_ref[:, place, :, cols] = y[r * 128 : (r + 1) * 128].reshape(4, 32, 256)


def spread_kernel(x_ref, o_ref):
    acc = x_ref[0].astype(F32)
    for i in range(1, x_ref.shape[0]):
        acc = acc + x_ref[i].astype(F32)
    acc = acc.astype(BF16)
    for i in range(o_ref.shape[0]):
        o_ref[i] = acc


def back_kernel(x_ref, down_ref, down2_ref, o_ref, out_ref):
    width = o_ref.shape[3]
    c = lax.axis_index("c")
    yh = lax.axis_index("yh")
    for r in range(2):
        place = yh if r == 0 else 1 - yh
        out_ref[r * 128 : (r + 1) * 128, :] = x_ref[:, place].reshape(128, x_ref.shape[3])
    for w_ref, place in ((down_ref, c), (down2_ref, 1 - c)):
        y = dot(out_ref[...], w_ref[:width, :], ((1,), (1,))).astype(BF16)
        for r in range(2):
            o_ref[place, :, 16 * r : 16 * r + 16, :] = y[r * 128 : (r + 1) * 128].reshape(
                8, 16, width
            )


def join_kernel(a_ref, b_ref, after_ref, o_ref):
    cols = a_ref.shape[1]
    o_ref[:, :cols] = a_ref[...]
    o_ref[:, cols:] = b_ref[...]


def turn_kernel(a_ref, b_ref, after_ref, o_ref):
    rows = a_ref.shape[0]
    o_ref[:, :rows] = a_ref[...].T
    o_ref[:, rows:] = b_ref[...].T


def bars_kernel(x_ref, up_slope_ref, act_ref, o_ref):
    width = act_ref.shape[1]
    c = lax.axis_index("c")
    for r in range(2):
        place = c if r == 0 else 1 - c
        rows = slice(r * 32, (r + 1) * 32)
        back = x_ref[place, 0].astype(F32)
        for i in range(1, 8):
            back = back + x_ref[place, i].astype(F32)
        gate_bar = (back * up_slope_ref[rows]).astype(BF16)
        up_bar = (back * act_ref[rows]).astype(BF16)
        for i in range(8):
            o_ref[i, rows, :width] = gate_bar
            o_ref[i, rows, width:] = up_bar


def fisher_down_kernel(hid_ref, out_ref, joined_ref, probe_ref, o_ref, done_ref):
    feats = out_ref.shape[1]
    own = hid_ref[...].T
    other = joined_ref[:, feats:].T
    for j in range(4):
        cols = slice(j * 256, (j + 1) * 256)
        y = dot(own, out_ref[:, cols]) + dot(other, joined_ref[:, cols])
        o_ref[:, cols] = (probe_ref[:, cols].astype(F32) * y * TOKENS**-0.5).astype(BF16)
    done_ref[...] = joined_ref[:16, :128]


def fisher_kernel(tok_ref, bars_ref, probe_ref, after_ref, gate_ref, up_ref):
    width = gate_ref.shape[1]
    factor = TOKENS**-0.5
    bars = [bars_ref[:, 16 * q : 16 * q + 16, :].reshape(128, 2 * width) for q in range(4)]
    y = dot(tok_ref[...], jnp.concatenate(bars, axis=0))
    gate_ref[...] = (probe_ref[:, :width].astype(F32) * y[:, :width] * factor).astype(BF16)
    up_ref[...] = (probe_ref[:, width:].astype(F32) * y[:, width:] * factor).astype(BF16)


def fisher(tok, bars, stacked, after):
    rows = stacked.shape[0]
    width = stacked.shape[1] // 4
    block = 256
    weight = pl.BlockSpec((block, width), lambda i: (i, 0))
    return pl.pallas_call(
        fisher_kernel,
        grid=(rows // block,),
        out_shape=[jax.ShapeDtypeStruct((rows, width), BF16)] * 2,
        in_specs=[
            pl.BlockSpec((block, tok.shape[1]), lambda i: (i, 0)),
            pl.BlockSpec(bars.shape, lambda i: (0, 0, 0)),
            pl.BlockSpec((block, 2 * width), lambda i: (i, 1)),
            pl.BlockSpec(memory_space=pl.ANY),
        ],
        out_specs=[weight, weight],
        compiler_params=pltpu.CompilerParams(vmem_limit_bytes=16 * 2**20),
    )(tok, bars, stacked, after)


def on_device(
    tokens,
    gate_weight,
    up_weight,
    down_weight,
    gate_mask,
    up_mask,
    down_mask,
    probe_gate,
    probe_up,
    probe_down,
):
    width = gate_weight.shape[1]
    feats = tokens.shape[1]

    (mine,) = local(copies_kernel, [((16, 8, feats), BF16)], tokens)
    tok0 = exchange(mine, ("zl", "zh")).reshape(128, feats)
    (stacked,) = local(
        stack_kernel,
        [((feats, 4 * width), BF16)],
        gate_mask,
        up_mask,
        gate_weight,
        up_weight,
        probe_gate,
        probe_up,
        scalars=2,
    )
    (down,) = local(
        down_kernel, [((2 * width, feats), BF16)], down_mask, down_weight, probe_down, scalars=1
    )
    down2 = swap(down, "c")
    tok1 = swap(tok0, "yh")
    tok1, seen, seen2 = lax.optimization_barrier((tok1, stacked[:16, :128], down2[:16, :128]))
    pair = jnp.concatenate([tok0, tok1], axis=0)
    pair2 = swap(pair, "c")
    (partial,) = local(
        pre_kernel, [((8, 64, 4 * width), BF16)], pair, pair2, stacked, seen, seen2, after=2
    )
    pre = exchange(partial, TP)
    send, up_slope, act = local(
        gate_kernel,
        [((2, 8, 32, 2 * width), BF16), ((64, width), F32), ((64, width), F32)],
        pre,
    )
    both = exchange(send.reshape(16, 32, 2 * width), NEAR).reshape(2, 8, 32, 2 * width)
    term, hid, hid2 = local(
        term_kernel,
        [((4, 2, 32, feats), BF16), ((256, width), BF16), ((256, width), BF16)],
        both,
        down,
        down2,
    )
    term = exchange(term.reshape(8, 32, feats), ("zl", "yh"))
    (chunk,) = local(spread_kernel, [((4, 32, feats), BF16)], term)
    chunk = exchange(chunk, "zh")
    (chunk,) = local(spread_kernel, [((8, 32, feats), BF16)], chunk)
    chunk = exchange(chunk, ("zl", "yh")).reshape(4, 2, 32, feats)
    back, out = local(
        back_kernel, [((2, 8, 32, width), BF16), ((256, feats), BF16)], chunk, down, down2
    )
    back = exchange(back.reshape(16, 32, width), NEAR).reshape(2, 8, 32, width)
    (bars,) = local(bars_kernel, [((8, 64, 2 * width), BF16)], back, up_slope, act)
    joined, tok_t = (
        local(join_kernel, [((256, feats + width), BF16)], out, hid2, bars, after=1)[0],
        local(turn_kernel, [((feats, TOKENS), BF16)], pair, pair2, bars, after=1)[0],
    )
    bars = exchange(bars, TP)
    joined = swap(joined, "c")
    fisher_down, done = local(
        fisher_down_kernel,
        [(probe_down.shape, BF16), ((16, 128), BF16)],
        hid,
        out,
        joined,
        probe_down,
    )
    fisher_gate, fisher_up = fisher(tok_t, bars, stacked, done)
    return (fisher_gate, fisher_up, fisher_down)


def solution(mesh):
    fine = Mesh(mesh.devices.reshape(2, 4, 4, 2, 2, 4), DP + TP)
    col = P(TP, DP)
    row = P(DP, TP)
    return jax.shard_map(
        on_device,
        mesh=fine,
        in_specs=(row, col, col, row, col, col, row, col, col, row),
        out_specs=(col, col, row),
        check_vma=False,
    )
```

```python
import jax
import jax.numpy as jnp
from jax import lax
from jax.experimental import pallas as pl
from jax.experimental.pallas import tpu as pltpu
from jax.sharding import Mesh, PartitionSpec as P

D = 8192
HID = 16384
TOKENS = 512
BF16 = jnp.bfloat16
F32 = jnp.float32
DP = ("yh", "zh", "zl", "c")
TP = ("yl", "x")
NEAR = ("c", "yl", "x")


def swap(x, axis):
    return lax.ppermute(x, axis, [(0, 1), (1, 0)])


def exchange(pieces, axes):
    return lax.all_to_all(pieces, axes, 0, 0, tiled=True)


def dot(a, b, dims=((1,), (0,))):
    return lax.dot_general(a, b, (dims, ((), ())), preferred_element_type=F32)


def local(kernel, outs, *args, scalars=0, after=0):
    spec = pl.BlockSpec(memory_space=pltpu.VMEM)
    small = pl.BlockSpec(memory_space=pltpu.SMEM)
    unread = pl.BlockSpec(memory_space=pl.ANY)
    return pl.pallas_call(
        kernel,
        out_shape=[jax.ShapeDtypeStruct(shape, dtype) for shape, dtype in outs],
        in_specs=[small] * scalars + [spec] * (len(args) - scalars - after) + [unread] * after,
        out_specs=[spec] * len(outs),
        compiler_params=pltpu.CompilerParams(vmem_limit_bytes=4 * 2**20),
    )(*args)


def copies_kernel(x_ref, o_ref):
    for i in range(o_ref.shape[0]):
        o_ref[i] = x_ref[...]


def keep(mask_ref, w_ref, o_ref):
    for i in range(mask_ref.shape[0]):
        for j in range(mask_ref.shape[1]):
            block = (slice(i * 128, (i + 1) * 128), slice(j * 128, (j + 1) * 128))
            o_ref[block] = (w_ref[block].astype(F32) * mask_ref[i, j].astype(F32)).astype(BF16)


def stack_kernel(gmask_ref, umask_ref, gate_ref, up_ref, pgate_ref, pup_ref, o_ref):
    width = gate_ref.shape[1]
    keep(gmask_ref, gate_ref, o_ref.at[:, :width])
    keep(umask_ref, up_ref, o_ref.at[:, width : 2 * width])
    o_ref[:, 2 * width : 3 * width] = pgate_ref[...]
    o_ref[:, 3 * width :] = pup_ref[...]


def pre_kernel(own_ref, other_ref, w_ref, *refs):
    o_ref = refs[-1]
    width = w_ref.shape[1] // 4
    for half, tok_ref in enumerate((own_ref, other_ref)):
        for j in range(4):
            cols = slice(j * width, (j + 1) * width)
            y = dot(tok_ref[...], w_ref[:, cols]).astype(BF16)
            for r in range(2):
                q = 16 * (2 * half + r)
                o_ref[:, q : q + 16, cols] = y[r * 128 : (r + 1) * 128].reshape(8, 16, width)


def down_kernel(mask_ref, down_ref, probe_ref, o_ref):
    width = down_ref.shape[0]
    keep(mask_ref, down_ref, o_ref.at[:width, :])
    o_ref[width:, :] = probe_ref[...]


def gate_kernel(x_ref, o_ref, up_slope_ref, act_ref):
    width = act_ref.shape[1]

    def part(j):
        cols = slice(j * width, (j + 1) * width)
        acc = x_ref[0, :, cols].astype(F32)
        for i in range(1, 8):
            acc = acc + x_ref[i, :, cols].astype(F32)
        return acc

    gate = part(0)
    up = part(1)
    tangent_gate = part(2) * D**-0.5
    tangent_up = part(3) * D**-0.5
    sig = jax.nn.sigmoid(gate)
    act = gate * sig
    slope = sig * (1.0 + gate * (1.0 - sig))
    hid = (act * up).astype(BF16)
    tan = (slope * tangent_gate * up + act * tangent_up).astype(BF16)
    c = lax.axis_index("c")
    for r in range(2):
        rows = slice(r * 32, (r + 1) * 32)
        place = c if r == 0 else 1 - c
        for i in range(8):
            o_ref[place, i, :, :width] = tan[rows]
            o_ref[place, i, :, width:] = hid[rows]
    up_slope_ref[...] = up * slope
    act_ref[...] = act


def term_kernel(x_ref, down_ref, down2_ref, o_ref, hid_ref, hid2_ref):
    width = hid_ref.shape[1]
    c = lax.axis_index("c")
    yh = lax.axis_index("yh")

    def rows(src):
        parts = [x_ref[src, :, 16 * r : 16 * r + 16, :].reshape(128, 2 * width) for r in range(2)]
        return jnp.concatenate(parts, axis=0)

    own = rows(c)
    other = rows(1 - c)
    hid_ref[...] = own[:, width:]
    hid2_ref[...] = other[:, width:]
    for j in range(4):
        cols = slice(j * 256, (j + 1) * 256)
        y = dot(own[:, width:], down_ref[width:, cols]) + dot(other[:, width:], down2_ref[width:, cols])
        y = y * HID**-0.5
        y = y + dot(own[:, :width], down_ref[:width, cols])
        y = y + dot(other[:, :width], down2_ref[:width, cols])
        y = y.astype(BF16)
        for r in range(2):
            place = yh if r == 0 else 1 - yh
            o_ref[:, place, :, cols] = y[r * 128 : (r + 1) * 128].reshape(4, 32, 256)


def spread_kernel(x_ref, o_ref):
    acc = x_ref[0].astype(F32)
    for i in range(1, x_ref.shape[0]):
        acc = acc + x_ref[i].astype(F32)
    acc = acc.astype(BF16)
    for i in range(o_ref.shape[0]):
        o_ref[i] = acc


def back_kernel(x_ref, down_ref, down2_ref, o_ref, out_ref):
    width = o_ref.shape[3]
    c = lax.axis_index("c")
    yh = lax.axis_index("yh")
    for r in range(2):
        place = yh if r == 0 else 1 - yh
        out_ref[r * 128 : (r + 1) * 128, :] = x_ref[:, place].reshape(128, x_ref.shape[3])
    for w_ref, place in ((down_ref, c), (down2_ref, 1 - c)):
        y = dot(out_ref[...], w_ref[:width, :], ((1,), (1,))).astype(BF16)
        for r in range(2):
            o_ref[place, :, 16 * r : 16 * r + 16, :] = y[r * 128 : (r + 1) * 128].reshape(
                8, 16, width
            )


def turn_kernel(a_ref, b_ref, after_ref, o_ref):
    rows = a_ref.shape[0]
    o_ref[:, :rows] = a_ref[...].T
    o_ref[:, rows:] = b_ref[...].T


def bars_kernel(x_ref, up_slope_ref, act_ref, out_ref, hid_ref, o_ref, joined_ref):
    width = act_ref.shape[1]
    feats = out_ref.shape[1]
    joined_ref[:, :feats] = out_ref[...]
    joined_ref[:, feats:] = hid_ref[...]
    c = lax.axis_index("c")
    for r in range(2):
        place = c if r == 0 else 1 - c
        rows = slice(r * 32, (r + 1) * 32)
        back = x_ref[place, 0].astype(F32)
        for i in range(1, 8):
            back = back + x_ref[place, i].astype(F32)
        gate_bar = (back * up_slope_ref[rows]).astype(BF16)
        up_bar = (back * act_ref[rows]).astype(BF16)
        for i in range(8):
            o_ref[i, rows, :width] = gate_bar
            o_ref[i, rows, width:] = up_bar


def fisher_down_kernel(hid_ref, out_ref, joined_ref, probe_ref, o_ref, done_ref):
    feats = out_ref.shape[1]
    own = hid_ref[...].T
    other = joined_ref[:, feats:].T
    for j in range(4):
        cols = slice(j * 256, (j + 1) * 256)
        y = dot(own, out_ref[:, cols]) + dot(other, joined_ref[:, cols])
        o_ref[:, cols] = (probe_ref[:, cols].astype(F32) * y * TOKENS**-0.5).astype(BF16)
    done_ref[...] = joined_ref[:16, :128]


def fisher_kernel(tok_ref, bars_ref, probe_ref, after_ref, gate_ref, up_ref, g_ref, u_ref, sem):
    width = gate_ref.shape[1]
    factor = TOKENS**-0.5
    bars = [bars_ref[:, 16 * q : 16 * q + 16, :].reshape(128, 2 * width) for q in range(4)]
    bars = jnp.concatenate(bars, axis=0)
    writes = []
    for i in range(4):
        rows = slice(i * 256, (i + 1) * 256)
        y = dot(tok_ref[rows, :], bars)
        for j, (held, target) in enumerate(((g_ref, gate_ref), (u_ref, up_ref))):
            probe = probe_ref[rows, (2 + j) * width : (3 + j) * width].astype(F32)
            held[rows, :] = (probe * y[:, j * width : (j + 1) * width] * factor).astype(BF16)
            write = pltpu.make_async_copy(held.at[rows, :], target.at[rows, :], sem.at[i, j])
            write.start()
            writes.append(write)
    for write in writes:
        write.wait()


def fisher(tok, bars, stacked, after):
    rows = stacked.shape[0]
    width = stacked.shape[1] // 4
    spec = pl.BlockSpec(memory_space=pltpu.VMEM)
    unread = pl.BlockSpec(memory_space=pl.ANY)
    return pl.pallas_call(
        fisher_kernel,
        out_shape=[jax.ShapeDtypeStruct((rows, width), BF16)] * 2,
        in_specs=[spec, spec, spec, unread],
        out_specs=[unread, unread],
        scratch_shapes=[
            pltpu.VMEM((rows, width), BF16),
            pltpu.VMEM((rows, width), BF16),
            pltpu.SemaphoreType.DMA((4, 2)),
        ],
        compiler_params=pltpu.CompilerParams(vmem_limit_bytes=8 * 2**20),
    )(tok, bars, stacked, after)


def on_device(
    tokens,
    gate_weight,
    up_weight,
    down_weight,
    gate_mask,
    up_mask,
    down_mask,
    probe_gate,
    probe_up,
    probe_down,
):
    width = gate_weight.shape[1]
    feats = tokens.shape[1]

    (mine,) = local(copies_kernel, [((16, 8, feats), BF16)], tokens)
    tok0 = exchange(mine, ("zl", "zh")).reshape(128, feats)
    (stacked,) = local(
        stack_kernel,
        [((feats, 4 * width), BF16)],
        gate_mask,
        up_mask,
        gate_weight,
        up_weight,
        probe_gate,
        probe_up,
        scalars=2,
    )
    (down,) = local(
        down_kernel, [((2 * width, feats), BF16)], down_mask, down_weight, probe_down, scalars=1
    )
    down2 = swap(down, "c")
    tok1 = swap(tok0, "yh")
    tok1, seen, seen2 = lax.optimization_barrier((tok1, stacked[:16, :128], down2[:16, :128]))
    pair = jnp.concatenate([tok0, tok1], axis=0)
    pair2 = swap(pair, "c")
    (partial,) = local(
        pre_kernel, [((8, 64, 4 * width), BF16)], pair, pair2, stacked, seen, seen2, after=2
    )
    pre = exchange(partial, TP)
    send, up_slope, act = local(
        gate_kernel,
        [((2, 8, 32, 2 * width), BF16), ((64, width), F32), ((64, width), F32)],
        pre,
    )
    both = exchange(send.reshape(16, 32, 2 * width), NEAR).reshape(2, 8, 32, 2 * width)
    term, hid, hid2 = local(
        term_kernel,
        [((4, 2, 32, feats), BF16), ((256, width), BF16), ((256, width), BF16)],
        both,
        down,
        down2,
    )
    term = exchange(term.reshape(8, 32, feats), ("zl", "yh"))
    (chunk,) = local(spread_kernel, [((4, 32, feats), BF16)], term)
    chunk = exchange(chunk, "zh")
    (chunk,) = local(spread_kernel, [((8, 32, feats), BF16)], chunk)
    chunk = exchange(chunk, ("zl", "yh")).reshape(4, 2, 32, feats)
    back, out = local(
        back_kernel, [((2, 8, 32, width), BF16), ((256, feats), BF16)], chunk, down, down2
    )
    back = exchange(back.reshape(16, 32, width), NEAR).reshape(2, 8, 32, width)
    bars, joined = local(
        bars_kernel,
        [((8, 64, 2 * width), BF16), ((256, feats + width), BF16)],
        back,
        up_slope,
        act,
        out,
        hid2,
    )
    (tok_t,) = local(turn_kernel, [((feats, TOKENS), BF16)], pair, pair2, bars, after=1)
    bars = exchange(bars, TP)
    joined = swap(joined, "c")
    fisher_down, done = local(
        fisher_down_kernel,
        [(probe_down.shape, BF16), ((16, 128), BF16)],
        hid,
        out,
        joined,
        probe_down,
    )
    fisher_gate, fisher_up = fisher(tok_t, bars, stacked, done)
    return (fisher_gate, fisher_up, fisher_down)


def solution(mesh):
    fine = Mesh(mesh.devices.reshape(2, 4, 4, 2, 2, 4), DP + TP)
    col = P(TP, DP)
    row = P(DP, TP)
    return jax.shard_map(
        on_device,
        mesh=fine,
        in_specs=(row, col, col, row, col, col, row, col, col, row),
        out_specs=(col, col, row),
        check_vma=False,
    )
```

```python
import jax
import jax.numpy as jnp
from jax import lax
from jax.experimental import pallas as pl
from jax.experimental.pallas import tpu as pltpu
from jax.sharding import Mesh, PartitionSpec as P

D = 8192
HID = 16384
TOKENS = 512
BF16 = jnp.bfloat16
F32 = jnp.float32
DP = ("yh", "zh", "zl", "c")
TP = ("yl", "x")
NEAR = ("c", "yl", "x")


def swap(x, axis):
    return lax.ppermute(x, axis, [(0, 1), (1, 0)])


def exchange(pieces, axes):
    return lax.all_to_all(pieces, axes, 0, 0, tiled=True)


def dot(a, b, dims=((1,), (0,))):
    return lax.dot_general(a, b, (dims, ((), ())), preferred_element_type=F32)


def local(kernel, outs, *args, scalars=0, after=0):
    spec = pl.BlockSpec(memory_space=pltpu.VMEM)
    small = pl.BlockSpec(memory_space=pltpu.SMEM)
    unread = pl.BlockSpec(memory_space=pl.ANY)
    return pl.pallas_call(
        kernel,
        out_shape=[jax.ShapeDtypeStruct(shape, dtype) for shape, dtype in outs],
        in_specs=[small] * scalars + [spec] * (len(args) - scalars - after) + [unread] * after,
        out_specs=[spec] * len(outs),
        compiler_params=pltpu.CompilerParams(vmem_limit_bytes=12 * 2**20),
    )(*args)


def copies_kernel(x_ref, o_ref):
    for i in range(o_ref.shape[0]):
        o_ref[i] = x_ref[...]


def keep(mask_ref, w_ref, o_ref):
    for i in range(mask_ref.shape[0]):
        for j in range(mask_ref.shape[1]):
            block = (slice(i * 128, (i + 1) * 128), slice(j * 128, (j + 1) * 128))
            o_ref[block] = (w_ref[block].astype(F32) * mask_ref[i, j].astype(F32)).astype(BF16)


def stack_kernel(gmask_ref, umask_ref, gate_ref, up_ref, pgate_ref, pup_ref, o_ref):
    width = gate_ref.shape[1]
    keep(gmask_ref, gate_ref, o_ref.at[:, :width])
    keep(umask_ref, up_ref, o_ref.at[:, width : 2 * width])
    o_ref[:, 2 * width : 3 * width] = pgate_ref[...]
    o_ref[:, 3 * width :] = pup_ref[...]


def pre_kernel(a_ref, b_ref, w_ref, w2_ref, after_ref, o_ref):
    width = w_ref.shape[1] // 4
    c = lax.axis_index("c")
    tok = jnp.concatenate([a_ref[...], b_ref[...]], axis=0)
    for weights, place in ((w_ref, c), (w2_ref, 1 - c)):
        for j in range(4):
            cols = slice(j * width, (j + 1) * width)
            y = dot(tok, weights[:, cols]).astype(BF16)
            for r in range(2):
                o_ref[place, :, 16 * r : 16 * r + 16, cols] = y[r * 128 : (r + 1) * 128].reshape(
                    8, 16, width
                )


def down_kernel(mask_ref, down_ref, probe_ref, o_ref):
    width = down_ref.shape[0]
    keep(mask_ref, down_ref, o_ref.at[:width, :])
    o_ref[width:, :] = probe_ref[...]


def gate_kernel(x_ref, o_ref, up_slope_ref, act_ref):
    width = act_ref.shape[1]

    c = lax.axis_index("c")

    def part(j):
        cols = slice(j * width, (j + 1) * width)
        classes = []
        for place in (c, 1 - c):
            acc = x_ref[place, 0, :, cols].astype(F32)
            for i in range(1, 8):
                acc = acc + x_ref[place, i, :, cols].astype(F32)
            classes.append(acc)
        return jnp.concatenate(classes, axis=0)

    gate = part(0)
    up = part(1)
    tangent_gate = part(2) * D**-0.5
    tangent_up = part(3) * D**-0.5
    sig = jax.nn.sigmoid(gate)
    act = gate * sig
    slope = sig * (1.0 + gate * (1.0 - sig))
    hid = (act * up).astype(BF16)
    tan = (slope * tangent_gate * up + act * tangent_up).astype(BF16)
    for r in range(2):
        rows = slice(r * 32, (r + 1) * 32)
        place = c if r == 0 else 1 - c
        for i in range(8):
            o_ref[place, i, :, :width] = tan[rows]
            o_ref[place, i, :, width:] = hid[rows]
    up_slope_ref[...] = up * slope
    act_ref[...] = act


def term_kernel(x_ref, down_ref, down2_ref, o_ref, hid_ref, hid2_ref):
    width = hid_ref.shape[1]
    c = lax.axis_index("c")
    yh = lax.axis_index("yh")

    def rows(src):
        parts = [x_ref[src, :, 16 * r : 16 * r + 16, :].reshape(128, 2 * width) for r in range(2)]
        return jnp.concatenate(parts, axis=0)

    own = rows(c)
    other = rows(1 - c)
    hid_ref[...] = own[:, width:]
    hid2_ref[...] = other[:, width:]
    for j in range(4):
        cols = slice(j * 256, (j + 1) * 256)
        y = dot(own[:, width:], down_ref[width:, cols]) + dot(other[:, width:], down2_ref[width:, cols])
        y = y * HID**-0.5
        y = y + dot(own[:, :width], down_ref[:width, cols])
        y = y + dot(other[:, :width], down2_ref[:width, cols])
        y = y.astype(BF16)
        for r in range(2):
            place = yh if r == 0 else 1 - yh
            o_ref[:, place, :, cols] = y[r * 128 : (r + 1) * 128].reshape(4, 32, 256)


def spread_kernel(x_ref, o_ref):
    acc = x_ref[0].astype(F32)
    for i in range(1, x_ref.shape[0]):
        acc = acc + x_ref[i].astype(F32)
    acc = acc.astype(BF16)
    for i in range(o_ref.shape[0]):
        o_ref[i] = acc


def back_kernel(x_ref, down_ref, down2_ref, o_ref, out_ref):
    width = o_ref.shape[3]
    c = lax.axis_index("c")
    yh = lax.axis_index("yh")
    for r in range(2):
        place = yh if r == 0 else 1 - yh
        out_ref[r * 128 : (r + 1) * 128, :] = x_ref[:, place].reshape(128, x_ref.shape[3])
    for w_ref, place in ((down_ref, c), (down2_ref, 1 - c)):
        y = dot(out_ref[...], w_ref[:width, :], ((1,), (1,))).astype(BF16)
        for r in range(2):
            o_ref[place, :, 16 * r : 16 * r + 16, :] = y[r * 128 : (r + 1) * 128].reshape(
                8, 16, width
            )


def turn_kernel(a_ref, b_ref, joined_ref, o_ref):
    feats, rows = a_ref.shape[1], a_ref.shape[0]
    o_ref[:, :rows] = a_ref[...].T
    o_ref[:, rows : 2 * rows] = b_ref[...].T
    o_ref[:, 2 * rows :] = joined_ref[:, -feats:].T


def bars_kernel(
    x_ref, up_slope_ref, act_ref, out_ref, hid_ref, a_ref, b_ref, o_ref, joined_ref
):
    width = act_ref.shape[1]
    feats = out_ref.shape[1]
    joined_ref[:, :feats] = out_ref[...]
    joined_ref[:, feats : feats + width] = hid_ref[...]
    joined_ref[:128, feats + width :] = a_ref[...]
    joined_ref[128:, feats + width :] = b_ref[...]
    c = lax.axis_index("c")
    for r in range(2):
        place = c if r == 0 else 1 - c
        rows = slice(r * 32, (r + 1) * 32)
        back = x_ref[place, 0].astype(F32)
        for i in range(1, 8):
            back = back + x_ref[place, i].astype(F32)
        gate_bar = (back * up_slope_ref[rows]).astype(BF16)
        up_bar = (back * act_ref[rows]).astype(BF16)
        for i in range(8):
            o_ref[i, rows, :width] = gate_bar
            o_ref[i, rows, width:] = up_bar


def fisher_down_kernel(hid_ref, out_ref, joined_ref, probe_ref, o_ref, done_ref):
    feats = out_ref.shape[1]
    own = hid_ref[...].T
    other = joined_ref[:, feats : feats + hid_ref.shape[1]].T
    for j in range(4):
        cols = slice(j * 256, (j + 1) * 256)
        y = dot(own, out_ref[:, cols]) + dot(other, joined_ref[:, cols])
        o_ref[:, cols] = (probe_ref[:, cols].astype(F32) * y * TOKENS**-0.5).astype(BF16)
    done_ref[...] = joined_ref[:16, :128]


def fisher_kernel(tok_ref, bars_ref, probe_ref, after_ref, gate_ref, up_ref, g_ref, u_ref, sem):
    width = gate_ref.shape[1]
    factor = TOKENS**-0.5
    bars = [bars_ref[:, 16 * q : 16 * q + 16, :].reshape(128, 2 * width) for q in range(4)]
    bars = jnp.concatenate(bars, axis=0)
    writes = []
    for i in range(4):
        rows = slice(i * 256, (i + 1) * 256)
        y = dot(tok_ref[rows, :], bars)
        for j, (held, target) in enumerate(((g_ref, gate_ref), (u_ref, up_ref))):
            probe = probe_ref[rows, (2 + j) * width : (3 + j) * width].astype(F32)
            held[rows, :] = (probe * y[:, j * width : (j + 1) * width] * factor).astype(BF16)
            write = pltpu.make_async_copy(held.at[rows, :], target.at[rows, :], sem.at[i, j])
            write.start()
            writes.append(write)
    for write in writes:
        write.wait()


def fisher(tok, bars, stacked, after):
    rows = stacked.shape[0]
    width = stacked.shape[1] // 4
    spec = pl.BlockSpec(memory_space=pltpu.VMEM)
    unread = pl.BlockSpec(memory_space=pl.ANY)
    return pl.pallas_call(
        fisher_kernel,
        out_shape=[jax.ShapeDtypeStruct((rows, width), BF16)] * 2,
        in_specs=[spec, spec, spec, unread],
        out_specs=[unread, unread],
        scratch_shapes=[
            pltpu.VMEM((rows, width), BF16),
            pltpu.VMEM((rows, width), BF16),
            pltpu.SemaphoreType.DMA((4, 2)),
        ],
        compiler_params=pltpu.CompilerParams(vmem_limit_bytes=12 * 2**20),
    )(tok, bars, stacked, after)


def on_device(
    tokens,
    gate_weight,
    up_weight,
    down_weight,
    gate_mask,
    up_mask,
    down_mask,
    probe_gate,
    probe_up,
    probe_down,
):
    width = gate_weight.shape[1]
    feats = tokens.shape[1]

    (mine,) = local(copies_kernel, [((16, 8, feats), BF16)], tokens)
    tok0 = exchange(mine, ("zl", "zh")).reshape(128, feats)
    (stacked,) = local(
        stack_kernel,
        [((feats, 4 * width), BF16)],
        gate_mask,
        up_mask,
        gate_weight,
        up_weight,
        probe_gate,
        probe_up,
        scalars=2,
    )
    (down,) = local(
        down_kernel, [((2 * width, feats), BF16)], down_mask, down_weight, probe_down, scalars=1
    )
    down2 = swap(down, "c")
    tok1 = swap(tok0, "yh")
    stacked2 = swap(stacked, "c")
    (partial,) = local(
        pre_kernel,
        [((2, 8, 32, 4 * width), BF16)],
        tok0,
        tok1,
        stacked,
        stacked2,
        down2,
        after=1,
    )
    pre = exchange(partial.reshape(16, 32, 4 * width), NEAR).reshape(2, 8, 32, 4 * width)
    send, up_slope, act = local(
        gate_kernel,
        [((2, 8, 32, 2 * width), BF16), ((64, width), F32), ((64, width), F32)],
        pre,
    )
    both = exchange(send.reshape(16, 32, 2 * width), NEAR).reshape(2, 8, 32, 2 * width)
    term, hid, hid2 = local(
        term_kernel,
        [((4, 2, 32, feats), BF16), ((256, width), BF16), ((256, width), BF16)],
        both,
        down,
        down2,
    )
    term = exchange(term.reshape(8, 32, feats), ("zl", "yh"))
    (chunk,) = local(spread_kernel, [((4, 32, feats), BF16)], term)
    chunk = exchange(chunk, "zh")
    (chunk,) = local(spread_kernel, [((8, 32, feats), BF16)], chunk)
    chunk = exchange(chunk, ("zl", "yh")).reshape(4, 2, 32, feats)
    back, out = local(
        back_kernel, [((2, 8, 32, width), BF16), ((256, feats), BF16)], chunk, down, down2
    )
    back = exchange(back.reshape(16, 32, width), NEAR).reshape(2, 8, 32, width)
    bars, joined = local(
        bars_kernel,
        [((8, 64, 2 * width), BF16), ((256, 2 * feats + width), BF16)],
        back,
        up_slope,
        act,
        out,
        hid2,
        tok0,
        tok1,
    )
    bars = exchange(bars, TP)
    joined = swap(joined, "c")
    (tok_t,) = local(turn_kernel, [((feats, TOKENS), BF16)], tok0, tok1, joined)
    fisher_down, done = local(
        fisher_down_kernel,
        [(probe_down.shape, BF16), ((16, 128), BF16)],
        hid,
        out,
        joined,
        probe_down,
    )
    fisher_gate, fisher_up = fisher(tok_t, bars, stacked, done)
    return (fisher_gate, fisher_up, fisher_down)


def solution(mesh):
    fine = Mesh(mesh.devices.reshape(2, 4, 4, 2, 2, 4), DP + TP)
    col = P(TP, DP)
    row = P(DP, TP)
    return jax.shard_map(
        on_device,
        mesh=fine,
        in_specs=(row, col, col, row, col, col, row, col, col, row),
        out_specs=(col, col, row),
        check_vma=False,
    )
```

```python
import jax
import jax.numpy as jnp
from jax import lax
from jax.experimental import pallas as pl
from jax.experimental.pallas import tpu as pltpu
from jax.sharding import Mesh, PartitionSpec as P

D = 8192
HID = 16384
TOKENS = 512
BF16 = jnp.bfloat16
F32 = jnp.float32
DP = ("yh", "zh", "zl", "c")
TP = ("yl", "x")
NEAR = ("c", "yl", "x")


def swap(x, axis):
    return lax.ppermute(x, axis, [(0, 1), (1, 0)])


def exchange(pieces, axes):
    return lax.all_to_all(pieces, axes, 0, 0, tiled=True)


def dot(a, b, dims=((1,), (0,))):
    return lax.dot_general(a, b, (dims, ((), ())), preferred_element_type=F32)


def local(kernel, outs, *args, scalars=0, after=0):
    spec = pl.BlockSpec(memory_space=pltpu.VMEM)
    small = pl.BlockSpec(memory_space=pltpu.SMEM)
    unread = pl.BlockSpec(memory_space=pl.ANY)
    return pl.pallas_call(
        kernel,
        out_shape=[jax.ShapeDtypeStruct(shape, dtype) for shape, dtype in outs],
        in_specs=[small] * scalars + [spec] * (len(args) - scalars - after) + [unread] * after,
        out_specs=[spec] * len(outs),
        compiler_params=pltpu.CompilerParams(vmem_limit_bytes=16 * 2**20),
    )(*args)


def copies_kernel(x_ref, o_ref):
    for i in range(o_ref.shape[0]):
        o_ref[i] = x_ref[...]


def keep(mask_ref, w_ref, o_ref):
    for i in range(mask_ref.shape[0]):
        for j in range(mask_ref.shape[1]):
            block = (slice(i * 128, (i + 1) * 128), slice(j * 128, (j + 1) * 128))
            o_ref[block] = (w_ref[block].astype(F32) * mask_ref[i, j].astype(F32)).astype(BF16)


def stack_kernel(gmask_ref, umask_ref, gate_ref, up_ref, pgate_ref, pup_ref, o_ref):
    width = gate_ref.shape[1]
    keep(gmask_ref, gate_ref, o_ref.at[:, :width])
    keep(umask_ref, up_ref, o_ref.at[:, width : 2 * width])
    o_ref[:, 2 * width : 3 * width] = pgate_ref[...]
    o_ref[:, 3 * width :] = pup_ref[...]


def pair_kernel(a_ref, b_ref, after_ref, after2_ref, o_ref):
    rows = a_ref.shape[0]
    o_ref[:rows] = a_ref[...]
    o_ref[rows:] = b_ref[...]


def pre_kernel(own_ref, other_ref, w_ref, o_ref):
    width = w_ref.shape[1] // 4
    for half, tok_ref in enumerate((own_ref, other_ref)):
        for j in range(4):
            cols = slice(j * width, (j + 1) * width)
            y = dot(tok_ref[...], w_ref[:, cols]).astype(BF16)
            for r in range(2):
                q = 16 * (2 * half + r)
                o_ref[:, q : q + 16, cols] = y[r * 128 : (r + 1) * 128].reshape(8, 16, width)


def down_kernel(mask_ref, down_ref, probe_ref, o_ref):
    width = down_ref.shape[0]
    keep(mask_ref, down_ref, o_ref.at[:width, :])
    o_ref[width:, :] = probe_ref[...]


def gate_kernel(x_ref, o_ref, up_slope_ref, act_ref):
    width = act_ref.shape[1]

    def part(j):
        cols = slice(j * width, (j + 1) * width)
        acc = x_ref[0, :, cols].astype(F32)
        for i in range(1, 8):
            acc = acc + x_ref[i, :, cols].astype(F32)
        return acc

    gate = part(0)
    up = part(1)
    tangent_gate = part(2) * D**-0.5
    tangent_up = part(3) * D**-0.5
    sig = jax.nn.sigmoid(gate)
    act = gate * sig
    slope = sig * (1.0 + gate * (1.0 - sig))
    hid = (act * up).astype(BF16)
    tan = (slope * tangent_gate * up + act * tangent_up).astype(BF16)
    c = lax.axis_index("c")
    for r in range(2):
        rows = slice(r * 32, (r + 1) * 32)
        place = c if r == 0 else 1 - c
        for i in range(8):
            o_ref[place, i, :, :width] = tan[rows]
            o_ref[place, i, :, width:] = hid[rows]
    up_slope_ref[...] = up * slope
    act_ref[...] = act


def term_kernel(x_ref, down_ref, down2_ref, o_ref, hid_ref, hid2_ref):
    width = hid_ref.shape[1]
    c = lax.axis_index("c")
    yh = lax.axis_index("yh")

    def rows(src):
        parts = [x_ref[src, :, 16 * r : 16 * r + 16, :].reshape(128, 2 * width) for r in range(2)]
        return jnp.concatenate(parts, axis=0)

    own = rows(c)
    other = rows(1 - c)
    hid_ref[...] = own[:, width:]
    hid2_ref[...] = other[:, width:]
    for j in range(4):
        cols = slice(j * 256, (j + 1) * 256)
        y = dot(own[:, width:], down_ref[width:, cols]) + dot(other[:, width:], down2_ref[width:, cols])
        y = y * HID**-0.5
        y = y + dot(own[:, :width], down_ref[:width, cols])
        y = y + dot(other[:, :width], down2_ref[:width, cols])
        y = y.astype(BF16)
        for r in range(2):
            place = yh if r == 0 else 1 - yh
            o_ref[:, place, :, cols] = y[r * 128 : (r + 1) * 128].reshape(4, 32, 256)


def spread_kernel(x_ref, o_ref):
    acc = x_ref[0].astype(F32)
    for i in range(1, x_ref.shape[0]):
        acc = acc + x_ref[i].astype(F32)
    acc = acc.astype(BF16)
    for i in range(o_ref.shape[0]):
        o_ref[i] = acc


def back_kernel(x_ref, down_ref, down2_ref, o_ref, out_ref):
    width = o_ref.shape[3]
    c = lax.axis_index("c")
    yh = lax.axis_index("yh")
    for r in range(2):
        place = yh if r == 0 else 1 - yh
        out_ref[r * 128 : (r + 1) * 128, :] = x_ref[:, place].reshape(128, x_ref.shape[3])
    for w_ref, place in ((down_ref, c), (down2_ref, 1 - c)):
        y = dot(out_ref[...], w_ref[:width, :], ((1,), (1,))).astype(BF16)
        for r in range(2):
            o_ref[place, :, 16 * r : 16 * r + 16, :] = y[r * 128 : (r + 1) * 128].reshape(
                8, 16, width
            )


def turn_kernel(a_ref, b_ref, after_ref, o_ref):
    rows = a_ref.shape[0]
    o_ref[:, :rows] = a_ref[...].T
    o_ref[:, rows:] = b_ref[...].T


def bars_kernel(x_ref, up_slope_ref, act_ref, out_ref, o_ref, late_ref):
    width = act_ref.shape[1]
    late_ref[...] = out_ref[...]
    c = lax.axis_index("c")
    for r in range(2):
        place = c if r == 0 else 1 - c
        rows = slice(r * 32, (r + 1) * 32)
        back = x_ref[place, 0].astype(F32)
        for i in range(1, 8):
            back = back + x_ref[place, i].astype(F32)
        gate_bar = (back * up_slope_ref[rows]).astype(BF16)
        up_bar = (back * act_ref[rows]).astype(BF16)
        for i in range(8):
            o_ref[i, rows, :width] = gate_bar
            o_ref[i, rows, width:] = up_bar


def fisher_down_kernel(hid_ref, out_ref, hid2_ref, out2_ref, probe_ref, o_ref, done_ref):
    own = hid_ref[...].T
    other = hid2_ref[...].T
    for j in range(4):
        cols = slice(j * 256, (j + 1) * 256)
        y = dot(own, out_ref[:, cols]) + dot(other, out2_ref[:, cols])
        o_ref[:, cols] = (probe_ref[:, cols].astype(F32) * y * TOKENS**-0.5).astype(BF16)
    done_ref[...] = out2_ref[:16, :128]


def fisher_kernel(tok_ref, bars_ref, probe_ref, after_ref, gate_ref, up_ref, g_ref, u_ref, sem):
    width = gate_ref.shape[1]
    factor = TOKENS**-0.5
    bars = [bars_ref[:, 16 * q : 16 * q + 16, :].reshape(128, 2 * width) for q in range(4)]
    bars = jnp.concatenate(bars, axis=0)
    writes = []
    for i in range(4):
        rows = slice(i * 256, (i + 1) * 256)
        y = dot(tok_ref[rows, :], bars)
        for j, (held, target) in enumerate(((g_ref, gate_ref), (u_ref, up_ref))):
            probe = probe_ref[rows, (2 + j) * width : (3 + j) * width].astype(F32)
            held[rows, :] = (probe * y[:, j * width : (j + 1) * width] * factor).astype(BF16)
            write = pltpu.make_async_copy(held.at[rows, :], target.at[rows, :], sem.at[i, j])
            write.start()
            writes.append(write)
    for write in writes:
        write.wait()


def fisher(tok, bars, stacked, after):
    rows = stacked.shape[0]
    width = stacked.shape[1] // 4
    spec = pl.BlockSpec(memory_space=pltpu.VMEM)
    unread = pl.BlockSpec(memory_space=pl.ANY)
    return pl.pallas_call(
        fisher_kernel,
        out_shape=[jax.ShapeDtypeStruct((rows, width), BF16)] * 2,
        in_specs=[spec, spec, spec, unread],
        out_specs=[unread, unread],
        scratch_shapes=[
            pltpu.VMEM((rows, width), BF16),
            pltpu.VMEM((rows, width), BF16),
            pltpu.SemaphoreType.DMA((4, 2)),
        ],
        compiler_params=pltpu.CompilerParams(vmem_limit_bytes=16 * 2**20),
    )(tok, bars, stacked, after)


def on_device(
    tokens,
    gate_weight,
    up_weight,
    down_weight,
    gate_mask,
    up_mask,
    down_mask,
    probe_gate,
    probe_up,
    probe_down,
):
    width = gate_weight.shape[1]
    feats = tokens.shape[1]

    (mine,) = local(copies_kernel, [((16, 8, feats), BF16)], tokens)
    tok0 = exchange(mine, ("zl", "zh")).reshape(128, feats)
    (stacked,) = local(
        stack_kernel,
        [((feats, 4 * width), BF16)],
        gate_mask,
        up_mask,
        gate_weight,
        up_weight,
        probe_gate,
        probe_up,
        scalars=2,
    )
    (down,) = local(
        down_kernel, [((2 * width, feats), BF16)], down_mask, down_weight, probe_down, scalars=1
    )
    down2 = swap(down, "c")
    tok1 = swap(tok0, "yh")
    (pair,) = local(pair_kernel, [((256, feats), BF16)], tok0, tok1, stacked, down2, after=2)
    pair2 = swap(pair, "c")
    (partial,) = local(pre_kernel, [((8, 64, 4 * width), BF16)], pair, pair2, stacked)
    pre = exchange(partial, TP)
    send, up_slope, act = local(
        gate_kernel,
        [((2, 8, 32, 2 * width), BF16), ((64, width), F32), ((64, width), F32)],
        pre,
    )
    both = exchange(send.reshape(16, 32, 2 * width), NEAR).reshape(2, 8, 32, 2 * width)
    term, hid, hid2 = local(
        term_kernel,
        [((4, 2, 32, feats), BF16), ((256, width), BF16), ((256, width), BF16)],
        both,
        down,
        down2,
    )
    term = exchange(term.reshape(8, 32, feats), ("zl", "yh"))
    (chunk,) = local(spread_kernel, [((4, 32, feats), BF16)], term)
    chunk = exchange(chunk, "zh")
    (chunk,) = local(spread_kernel, [((8, 32, feats), BF16)], chunk)
    chunk = exchange(chunk, ("zl", "yh")).reshape(4, 2, 32, feats)
    back, out = local(
        back_kernel, [((2, 8, 32, width), BF16), ((256, feats), BF16)], chunk, down, down2
    )
    back = exchange(back.reshape(16, 32, width), NEAR).reshape(2, 8, 32, width)
    bars, late = local(
        bars_kernel,
        [((8, 64, 2 * width), BF16), ((256, feats), BF16)],
        back,
        up_slope,
        act,
        out,
    )
    (tok_t,) = local(turn_kernel, [((feats, TOKENS), BF16)], pair, pair2, bars, after=1)
    bars = exchange(bars, TP)
    out2 = swap(late, "c")
    hid2 = swap(hid2, "c")
    fisher_down, done = local(
        fisher_down_kernel,
        [(probe_down.shape, BF16), ((16, 128), BF16)],
        hid,
        out,
        hid2,
        out2,
        probe_down,
    )
    fisher_gate, fisher_up = fisher(tok_t, bars, stacked, done)
    return (fisher_gate, fisher_up, fisher_down)


def solution(mesh):
    fine = Mesh(mesh.devices.reshape(2, 4, 4, 2, 2, 4), DP + TP)
    col = P(TP, DP)
    row = P(DP, TP)
    return jax.shard_map(
        on_device,
        mesh=fine,
        in_specs=(row, col, col, row, col, col, row, col, col, row),
        out_specs=(col, col, row),
        check_vma=False,
    )
```

```python
import jax
import jax.numpy as jnp
from jax import lax
from jax.experimental import pallas as pl
from jax.experimental.pallas import tpu as pltpu
from jax.sharding import Mesh, PartitionSpec as P

D = 8192
HID = 16384
TOKENS = 512
BF16 = jnp.bfloat16
F32 = jnp.float32
DP = ("yh", "zh", "zl", "c")
TP = ("yl", "x")
NEAR = ("c", "yl", "x")


def swap(x, axis):
    return lax.ppermute(x, axis, [(0, 1), (1, 0)])


def exchange(pieces, axes):
    return lax.all_to_all(pieces, axes, 0, 0, tiled=True)


def dot(a, b, dims=((1,), (0,))):
    return lax.dot_general(a, b, (dims, ((), ())), preferred_element_type=F32)


def local(kernel, outs, *args, scalars=0, after=0):
    spec = pl.BlockSpec(memory_space=pltpu.VMEM)
    small = pl.BlockSpec(memory_space=pltpu.SMEM)
    unread = pl.BlockSpec(memory_space=pl.ANY)
    return pl.pallas_call(
        kernel,
        out_shape=[jax.ShapeDtypeStruct(shape, dtype) for shape, dtype in outs],
        in_specs=[small] * scalars + [spec] * (len(args) - scalars - after) + [unread] * after,
        out_specs=[spec] * len(outs),
        compiler_params=pltpu.CompilerParams(vmem_limit_bytes=16 * 2**20),
    )(*args)


def copies_kernel(x_ref, o_ref):
    for i in range(o_ref.shape[0]):
        o_ref[i] = x_ref[...]


def keep(mask_ref, w_ref, o_ref):
    for i in range(mask_ref.shape[0]):
        for j in range(mask_ref.shape[1]):
            block = (slice(i * 128, (i + 1) * 128), slice(j * 128, (j + 1) * 128))
            o_ref[block] = (w_ref[block].astype(F32) * mask_ref[i, j].astype(F32)).astype(BF16)


def stack_kernel(gmask_ref, umask_ref, gate_ref, up_ref, pgate_ref, pup_ref, o_ref):
    width = gate_ref.shape[1]
    keep(gmask_ref, gate_ref, o_ref.at[:, :width])
    keep(umask_ref, up_ref, o_ref.at[:, width : 2 * width])
    o_ref[:, 2 * width : 3 * width] = pgate_ref[...]
    o_ref[:, 3 * width :] = pup_ref[...]


def pair_kernel(a_ref, b_ref, after_ref, after2_ref, o_ref):
    rows = a_ref.shape[0]
    o_ref[:rows] = a_ref[...]
    o_ref[rows:] = b_ref[...]


def hold_kernel(x_ref, after_ref, o_ref):
    o_ref[...] = x_ref[...]


def pre_kernel(own_ref, other_ref, w_ref, after_ref, o_ref, turned_ref):
    rows = own_ref.shape[0]
    turned_ref[:, :rows] = own_ref[...].T
    turned_ref[:, rows:] = other_ref[...].T
    width = w_ref.shape[1] // 4
    for half, tok_ref in enumerate((own_ref, other_ref)):
        for j in range(4):
            cols = slice(j * width, (j + 1) * width)
            y = dot(tok_ref[...], w_ref[:, cols]).astype(BF16)
            for r in range(2):
                q = 16 * (2 * half + r)
                o_ref[:, q : q + 16, cols] = y[r * 128 : (r + 1) * 128].reshape(8, 16, width)


def down_kernel(mask_ref, down_ref, probe_ref, o_ref):
    width = down_ref.shape[0]
    keep(mask_ref, down_ref, o_ref.at[:width, :])
    o_ref[width:, :] = probe_ref[...]


def gate_kernel(x_ref, o_ref, up_slope_ref, act_ref):
    width = act_ref.shape[1]

    def part(j):
        cols = slice(j * width, (j + 1) * width)
        acc = x_ref[0, :, cols].astype(F32)
        for i in range(1, 8):
            acc = acc + x_ref[i, :, cols].astype(F32)
        return acc

    gate = part(0)
    up = part(1)
    tangent_gate = part(2) * D**-0.5
    tangent_up = part(3) * D**-0.5
    sig = jax.nn.sigmoid(gate)
    act = gate * sig
    slope = sig * (1.0 + gate * (1.0 - sig))
    hid = (act * up).astype(BF16)
    tan = (slope * tangent_gate * up + act * tangent_up).astype(BF16)
    c = lax.axis_index("c")
    for r in range(2):
        rows = slice(r * 32, (r + 1) * 32)
        place = c if r == 0 else 1 - c
        for i in range(8):
            o_ref[place, i, :, :width] = tan[rows]
            o_ref[place, i, :, width:] = hid[rows]
    up_slope_ref[...] = up * slope
    act_ref[...] = act


def term_kernel(x_ref, down_ref, down2_ref, o_ref, hid_ref, hid2_ref):
    width = hid_ref.shape[1]
    c = lax.axis_index("c")
    yh = lax.axis_index("yh")

    def rows(src):
        parts = [x_ref[src, :, 16 * r : 16 * r + 16, :].reshape(128, 2 * width) for r in range(2)]
        return jnp.concatenate(parts, axis=0)

    own = rows(c)
    other = rows(1 - c)
    hid_ref[...] = own[:, width:]
    hid2_ref[...] = other[:, width:]
    for j in range(4):
        cols = slice(j * 256, (j + 1) * 256)
        y = dot(own[:, width:], down_ref[width:, cols]) + dot(other[:, width:], down2_ref[width:, cols])
        y = y * HID**-0.5
        y = y + dot(own[:, :width], down_ref[:width, cols])
        y = y + dot(other[:, :width], down2_ref[:width, cols])
        y = y.astype(BF16)
        for r in range(2):
            place = yh if r == 0 else 1 - yh
            o_ref[:, place, :, cols] = y[r * 128 : (r + 1) * 128].reshape(4, 32, 256)


def spread_kernel(x_ref, o_ref):
    acc = x_ref[0].astype(F32)
    for i in range(1, x_ref.shape[0]):
        acc = acc + x_ref[i].astype(F32)
    acc = acc.astype(BF16)
    for i in range(o_ref.shape[0]):
        o_ref[i] = acc


def back_kernel(x_ref, down_ref, down2_ref, o_ref, out_ref):
    width = o_ref.shape[3]
    c = lax.axis_index("c")
    yh = lax.axis_index("yh")
    for r in range(2):
        place = yh if r == 0 else 1 - yh
        out_ref[r * 128 : (r + 1) * 128, :] = x_ref[:, place].reshape(128, x_ref.shape[3])
    for w_ref, place in ((down_ref, c), (down2_ref, 1 - c)):
        y = dot(out_ref[...], w_ref[:width, :], ((1,), (1,))).astype(BF16)
        for r in range(2):
            o_ref[place, :, 16 * r : 16 * r + 16, :] = y[r * 128 : (r + 1) * 128].reshape(
                8, 16, width
            )


def bars_kernel(x_ref, up_slope_ref, act_ref, out_ref, o_ref, late_ref):
    width = act_ref.shape[1]
    late_ref[...] = out_ref[...]
    c = lax.axis_index("c")
    for r in range(2):
        place = c if r == 0 else 1 - c
        rows = slice(r * 32, (r + 1) * 32)
        back = x_ref[place, 0].astype(F32)
        for i in range(1, 8):
            back = back + x_ref[place, i].astype(F32)
        gate_bar = (back * up_slope_ref[rows]).astype(BF16)
        up_bar = (back * act_ref[rows]).astype(BF16)
        for i in range(8):
            o_ref[i, rows, :width] = gate_bar
            o_ref[i, rows, width:] = up_bar


def fisher_kernel(tok_ref, bars_ref, probe_ref, gate_ref, up_ref, g_ref, u_ref, sem):
    width = gate_ref.shape[1]
    factor = TOKENS**-0.5
    bars = [bars_ref[:, 16 * q : 16 * q + 16, :].reshape(128, 2 * width) for q in range(4)]
    bars = jnp.concatenate(bars, axis=0)
    writes = []
    for i in range(4):
        rows = slice(i * 256, (i + 1) * 256)
        y = dot(tok_ref[rows, :], bars)
        for j, (held, target) in enumerate(((g_ref, gate_ref), (u_ref, up_ref))):
            probe = probe_ref[rows, (2 + j) * width : (3 + j) * width].astype(F32)
            held[rows, :] = (probe * y[:, j * width : (j + 1) * width] * factor).astype(BF16)
            write = pltpu.make_async_copy(held.at[rows, :], target.at[rows, :], sem.at[i, j])
            write.start()
            writes.append(write)
    for write in writes:
        write.wait()


def fisher(tok, bars, stacked):
    rows = stacked.shape[0]
    width = stacked.shape[1] // 4
    spec = pl.BlockSpec(memory_space=pltpu.VMEM)
    unread = pl.BlockSpec(memory_space=pl.ANY)
    return pl.pallas_call(
        fisher_kernel,
        out_shape=[jax.ShapeDtypeStruct((rows, width), BF16)] * 2,
        in_specs=[spec, spec, spec],
        out_specs=[unread, unread],
        scratch_shapes=[
            pltpu.VMEM((rows, width), BF16),
            pltpu.VMEM((rows, width), BF16),
            pltpu.SemaphoreType.DMA((4, 2)),
        ],
        compiler_params=pltpu.CompilerParams(vmem_limit_bytes=16 * 2**20),
    )(tok, bars, stacked)


def on_device(
    tokens,
    gate_weight,
    up_weight,
    down_weight,
    gate_mask,
    up_mask,
    down_mask,
    probe_gate,
    probe_up,
    probe_down,
):
    width = gate_weight.shape[1]
    feats = tokens.shape[1]

    (mine,) = local(copies_kernel, [((16, 8, feats), BF16)], tokens)
    tok0 = exchange(mine, ("zl", "zh")).reshape(128, feats)
    (stacked,) = local(
        stack_kernel,
        [((feats, 4 * width), BF16)],
        gate_mask,
        up_mask,
        gate_weight,
        up_weight,
        probe_gate,
        probe_up,
        scalars=2,
    )
    (down,) = local(
        down_kernel, [((2 * width, feats), BF16)], down_mask, down_weight, probe_down, scalars=1
    )
    down2 = swap(down, "c")
    tok1 = swap(tok0, "yh")
    (pair,) = local(pair_kernel, [((256, feats), BF16)], tok0, tok1, stacked, down2, after=2)
    pair2 = swap(pair, "c")
    (down2,) = local(hold_kernel, [(down2.shape, BF16)], down2, pair, after=1)
    partial, tok_t = local(
        pre_kernel,
        [((8, 64, 4 * width), BF16), ((feats, TOKENS), BF16)],
        pair,
        pair2,
        stacked,
        down2,
        after=1,
    )
    pre = exchange(partial, TP)
    send, up_slope, act = local(
        gate_kernel,
        [((2, 8, 32, 2 * width), BF16), ((64, width), F32), ((64, width), F32)],
        pre,
    )
    both = exchange(send.reshape(16, 32, 2 * width), NEAR).reshape(2, 8, 32, 2 * width)
    term, hid, hid2 = local(
        term_kernel,
        [((4, 2, 32, feats), BF16), ((256, width), BF16), ((256, width), BF16)],
        both,
        down,
        down2,
    )
    term = exchange(term.reshape(8, 32, feats), ("zl", "yh"))
    (chunk,) = local(spread_kernel, [((4, 32, feats), BF16)], term)
    chunk = exchange(chunk, "zh")
    (chunk,) = local(spread_kernel, [((8, 32, feats), BF16)], chunk)
    chunk = exchange(chunk, ("zl", "yh")).reshape(4, 2, 32, feats)
    back, out = local(
        back_kernel, [((2, 8, 32, width), BF16), ((256, feats), BF16)], chunk, down, down2
    )
    back = exchange(back.reshape(16, 32, width), NEAR).reshape(2, 8, 32, width)
    bars, late = local(
        bars_kernel,
        [((8, 64, 2 * width), BF16), ((256, feats), BF16)],
        back,
        up_slope,
        act,
        out,
    )
    bars = exchange(bars, TP)
    out2 = swap(late, "c")
    hid2 = swap(hid2, "c")
    grad_down = dot(
        jnp.concatenate([hid, hid2], axis=0), jnp.concatenate([out, out2], axis=0), ((0,), (0,))
    )
    fisher_down = (probe_down.astype(F32) * grad_down * TOKENS**-0.5).astype(BF16)
    fisher_gate, fisher_up = fisher(tok_t, bars, stacked)
    return (fisher_gate, fisher_up, fisher_down)


def solution(mesh):
    fine = Mesh(mesh.devices.reshape(2, 4, 4, 2, 2, 4), DP + TP)
    col = P(TP, DP)
    row = P(DP, TP)
    return jax.shard_map(
        on_device,
        mesh=fine,
        in_specs=(row, col, col, row, col, col, row, col, col, row),
        out_specs=(col, col, row),
        check_vma=False,
    )
```

```python
import jax
import jax.numpy as jnp
from jax import lax
from jax.experimental import pallas as pl
from jax.experimental.pallas import tpu as pltpu
from jax.sharding import Mesh, PartitionSpec as P

D = 8192
HID = 16384
TOKENS = 512
BF16 = jnp.bfloat16
F32 = jnp.float32
DP = ("yh", "zh", "zl", "c")
TP = ("yl", "x")
NEAR = ("c", "yl", "x")


def swap(x, axis):
    return lax.ppermute(x, axis, [(0, 1), (1, 0)])


def exchange(pieces, axes):
    return lax.all_to_all(pieces, axes, 0, 0, tiled=True)


def dot(a, b, dims=((1,), (0,))):
    return lax.dot_general(a, b, (dims, ((), ())), preferred_element_type=F32)


def local(kernel, outs, *args, scalars=0, after=0):
    spec = pl.BlockSpec(memory_space=pltpu.VMEM)
    small = pl.BlockSpec(memory_space=pltpu.SMEM)
    unread = pl.BlockSpec(memory_space=pl.ANY)
    return pl.pallas_call(
        kernel,
        out_shape=[jax.ShapeDtypeStruct(shape, dtype) for shape, dtype in outs],
        in_specs=[small] * scalars + [spec] * (len(args) - scalars - after) + [unread] * after,
        out_specs=[spec] * len(outs),
        compiler_params=pltpu.CompilerParams(vmem_limit_bytes=16 * 2**20),
    )(*args)


def copies_kernel(x_ref, o_ref):
    for i in range(o_ref.shape[0]):
        o_ref[i] = x_ref[...]


def keep(mask_ref, w_ref, o_ref):
    for i in range(mask_ref.shape[0]):
        for j in range(mask_ref.shape[1]):
            block = (slice(i * 128, (i + 1) * 128), slice(j * 128, (j + 1) * 128))
            o_ref[block] = (w_ref[block].astype(F32) * mask_ref[i, j].astype(F32)).astype(BF16)


def stack_kernel(gmask_ref, umask_ref, gate_ref, up_ref, pgate_ref, pup_ref, o_ref):
    width = gate_ref.shape[1]
    keep(gmask_ref, gate_ref, o_ref.at[:, :width])
    keep(umask_ref, up_ref, o_ref.at[:, width : 2 * width])
    o_ref[:, 2 * width : 3 * width] = pgate_ref[...]
    o_ref[:, 3 * width :] = pup_ref[...]


def pair_kernel(a_ref, b_ref, after_ref, after2_ref, o_ref):
    rows = a_ref.shape[0]
    o_ref[:rows] = a_ref[...]
    o_ref[rows:] = b_ref[...]


def hold_kernel(x_ref, after_ref, o_ref):
    o_ref[...] = x_ref[...]


def pre_kernel(own_ref, other_ref, w_ref, after_ref, o_ref, turned_ref):
    rows = own_ref.shape[0]
    turned_ref[:, :rows] = own_ref[...].T
    turned_ref[:, rows:] = other_ref[...].T
    width = w_ref.shape[1] // 4
    for half, tok_ref in enumerate((own_ref, other_ref)):
        for j in range(4):
            cols = slice(j * width, (j + 1) * width)
            y = dot(tok_ref[...], w_ref[:, cols]).astype(BF16)
            for r in range(2):
                q = 16 * (2 * half + r)
                o_ref[:, q : q + 16, cols] = y[r * 128 : (r + 1) * 128].reshape(8, 16, width)


def down_kernel(mask_ref, down_ref, probe_ref, o_ref):
    width = down_ref.shape[0]
    keep(mask_ref, down_ref, o_ref.at[:width, :])
    o_ref[width:, :] = probe_ref[...]


def gate_kernel(x_ref, o_ref, up_slope_ref, act_ref):
    width = act_ref.shape[1]

    def part(j):
        cols = slice(j * width, (j + 1) * width)
        acc = x_ref[0, :, cols].astype(F32)
        for i in range(1, 8):
            acc = acc + x_ref[i, :, cols].astype(F32)
        return acc

    gate = part(0)
    up = part(1)
    tangent_gate = part(2) * D**-0.5
    tangent_up = part(3) * D**-0.5
    sig = jax.nn.sigmoid(gate)
    act = gate * sig
    slope = sig * (1.0 + gate * (1.0 - sig))
    hid = (act * up).astype(BF16)
    tan = (slope * tangent_gate * up + act * tangent_up).astype(BF16)
    c = lax.axis_index("c")
    for r in range(2):
        rows = slice(r * 32, (r + 1) * 32)
        place = c if r == 0 else 1 - c
        for i in range(8):
            o_ref[place, i, :, :width] = tan[rows]
            o_ref[place, i, :, width:] = hid[rows]
    up_slope_ref[...] = up * slope
    act_ref[...] = act


def term_kernel(x_ref, down_ref, down2_ref, o_ref, hid_ref, hid2_ref):
    width = hid_ref.shape[1]
    c = lax.axis_index("c")
    yh = lax.axis_index("yh")

    def rows(src):
        parts = [x_ref[src, :, 16 * r : 16 * r + 16, :].reshape(128, 2 * width) for r in range(2)]
        return jnp.concatenate(parts, axis=0)

    own = rows(c)
    other = rows(1 - c)
    hid_ref[...] = own[:, width:]
    hid2_ref[...] = other[:, width:]
    for j in range(4):
        cols = slice(j * 256, (j + 1) * 256)
        y = dot(own[:, width:], down_ref[width:, cols]) + dot(other[:, width:], down2_ref[width:, cols])
        y = y * HID**-0.5
        y = y + dot(own[:, :width], down_ref[:width, cols])
        y = y + dot(other[:, :width], down2_ref[:width, cols])
        y = y.astype(BF16)
        for r in range(2):
            place = yh if r == 0 else 1 - yh
            o_ref[:, place, :, cols] = y[r * 128 : (r + 1) * 128].reshape(4, 32, 256)


def spread_kernel(x_ref, o_ref):
    acc = x_ref[0].astype(F32)
    for i in range(1, x_ref.shape[0]):
        acc = acc + x_ref[i].astype(F32)
    acc = acc.astype(BF16)
    for i in range(o_ref.shape[0]):
        o_ref[i] = acc


def back_kernel(x_ref, down_ref, down2_ref, o_ref, out_ref):
    width = o_ref.shape[3]
    c = lax.axis_index("c")
    yh = lax.axis_index("yh")
    for r in range(2):
        place = yh if r == 0 else 1 - yh
        out_ref[r * 128 : (r + 1) * 128, :] = x_ref[:, place].reshape(128, x_ref.shape[3])
    for w_ref, place in ((down_ref, c), (down2_ref, 1 - c)):
        y = dot(out_ref[...], w_ref[:width, :], ((1,), (1,))).astype(BF16)
        for r in range(2):
            o_ref[place, :, 16 * r : 16 * r + 16, :] = y[r * 128 : (r + 1) * 128].reshape(
                8, 16, width
            )


def bars_kernel(x_ref, up_slope_ref, act_ref, out_ref, o_ref, late_ref, late2_ref):
    width = act_ref.shape[1]
    half = late_ref.shape[1]
    late_ref[...] = out_ref[:, :half]
    late2_ref[...] = out_ref[:, half:]
    c = lax.axis_index("c")
    for r in range(2):
        place = c if r == 0 else 1 - c
        rows = slice(r * 32, (r + 1) * 32)
        back = x_ref[place, 0].astype(F32)
        for i in range(1, 8):
            back = back + x_ref[place, i].astype(F32)
        gate_bar = (back * up_slope_ref[rows]).astype(BF16)
        up_bar = (back * act_ref[rows]).astype(BF16)
        for i in range(8):
            o_ref[i, rows, :width] = gate_bar
            o_ref[i, rows, width:] = up_bar


def fisher_down_kernel(
    hid_ref, out_ref, hid2_ref, late_ref, late2_ref, probe_ref, o_ref, done_ref
):
    own = hid_ref[...].T
    other = hid2_ref[...].T
    for j in range(4):
        cols = slice(j * 256, (j + 1) * 256)
        part = slice(j % 2 * 256, (j % 2 + 1) * 256)
        y = dot(own, out_ref[:, cols]) + dot(other, (late_ref, late2_ref)[j // 2][:, part])
        o_ref[:, cols] = (probe_ref[:, cols].astype(F32) * y * TOKENS**-0.5).astype(BF16)
    done_ref[...] = late2_ref[:16, :128]


def fisher_kernel(tok_ref, bars_ref, probe_ref, after_ref, gate_ref, up_ref, g_ref, u_ref, sem):
    width = gate_ref.shape[1]
    factor = TOKENS**-0.5
    bars = [bars_ref[:, 16 * q : 16 * q + 16, :].reshape(128, 2 * width) for q in range(4)]
    bars = jnp.concatenate(bars, axis=0)
    writes = []
    for i in range(4):
        rows = slice(i * 256, (i + 1) * 256)
        y = dot(tok_ref[rows, :], bars)
        for j, (held, target) in enumerate(((g_ref, gate_ref), (u_ref, up_ref))):
            probe = probe_ref[rows, (2 + j) * width : (3 + j) * width].astype(F32)
            held[rows, :] = (probe * y[:, j * width : (j + 1) * width] * factor).astype(BF16)
            write = pltpu.make_async_copy(held.at[rows, :], target.at[rows, :], sem.at[i, j])
            write.start()
            writes.append(write)
    for write in writes:
        write.wait()


def fisher(tok, bars, stacked, after):
    rows = stacked.shape[0]
    width = stacked.shape[1] // 4
    spec = pl.BlockSpec(memory_space=pltpu.VMEM)
    unread = pl.BlockSpec(memory_space=pl.ANY)
    return pl.pallas_call(
        fisher_kernel,
        out_shape=[jax.ShapeDtypeStruct((rows, width), BF16)] * 2,
        in_specs=[spec, spec, spec, unread],
        out_specs=[unread, unread],
        scratch_shapes=[
            pltpu.VMEM((rows, width), BF16),
            pltpu.VMEM((rows, width), BF16),
            pltpu.SemaphoreType.DMA((4, 2)),
        ],
        compiler_params=pltpu.CompilerParams(vmem_limit_bytes=16 * 2**20),
    )(tok, bars, stacked, after)


def on_device(
    tokens,
    gate_weight,
    up_weight,
    down_weight,
    gate_mask,
    up_mask,
    down_mask,
    probe_gate,
    probe_up,
    probe_down,
):
    width = gate_weight.shape[1]
    feats = tokens.shape[1]

    (mine,) = local(copies_kernel, [((16, 8, feats), BF16)], tokens)
    tok0 = exchange(mine, ("zl", "zh")).reshape(128, feats)
    (stacked,) = local(
        stack_kernel,
        [((feats, 4 * width), BF16)],
        gate_mask,
        up_mask,
        gate_weight,
        up_weight,
        probe_gate,
        probe_up,
        scalars=2,
    )
    (down,) = local(
        down_kernel, [((2 * width, feats), BF16)], down_mask, down_weight, probe_down, scalars=1
    )
    down2 = swap(down, "c")
    tok1 = swap(tok0, "yh")
    (pair,) = local(pair_kernel, [((256, feats), BF16)], tok0, tok1, stacked, down2, after=2)
    pair2 = swap(pair, "c")
    (down2,) = local(hold_kernel, [(down2.shape, BF16)], down2, pair, after=1)
    partial, tok_t = local(
        pre_kernel,
        [((8, 64, 4 * width), BF16), ((feats, TOKENS), BF16)],
        pair,
        pair2,
        stacked,
        down2,
        after=1,
    )
    pre = exchange(partial, TP)
    send, up_slope, act = local(
        gate_kernel,
        [((2, 8, 32, 2 * width), BF16), ((64, width), F32), ((64, width), F32)],
        pre,
    )
    both = exchange(send.reshape(16, 32, 2 * width), NEAR).reshape(2, 8, 32, 2 * width)
    term, hid, hid2 = local(
        term_kernel,
        [((4, 2, 32, feats), BF16), ((256, width), BF16), ((256, width), BF16)],
        both,
        down,
        down2,
    )
    term = exchange(term.reshape(8, 32, feats), ("zl", "yh"))
    (chunk,) = local(spread_kernel, [((4, 32, feats), BF16)], term)
    chunk = exchange(chunk, "zh")
    (chunk,) = local(spread_kernel, [((8, 32, feats), BF16)], chunk)
    chunk = exchange(chunk, ("zl", "yh")).reshape(4, 2, 32, feats)
    back, out = local(
        back_kernel, [((2, 8, 32, width), BF16), ((256, feats), BF16)], chunk, down, down2
    )
    back = exchange(back.reshape(16, 32, width), NEAR).reshape(2, 8, 32, width)
    bars, late, late2 = local(
        bars_kernel,
        [((8, 64, 2 * width), BF16), ((256, feats // 2), BF16), ((256, feats // 2), BF16)],
        back,
        up_slope,
        act,
        out,
    )
    bars = exchange(bars, TP)
    fisher_down, done = local(
        fisher_down_kernel,
        [(probe_down.shape, BF16), ((16, 128), BF16)],
        hid,
        out,
        swap(hid2, "c"),
        swap(late, "c"),
        swap(late2, "c"),
        probe_down,
    )
    fisher_gate, fisher_up = fisher(tok_t, bars, stacked, done)
    return (fisher_gate, fisher_up, fisher_down)


def solution(mesh):
    fine = Mesh(mesh.devices.reshape(2, 4, 4, 2, 2, 4), DP + TP)
    col = P(TP, DP)
    row = P(DP, TP)
    return jax.shard_map(
        on_device,
        mesh=fine,
        in_specs=(row, col, col, row, col, col, row, col, col, row),
        out_specs=(col, col, row),
        check_vma=False,
    )
```

```python
import jax
import jax.numpy as jnp
from jax import lax
from jax.experimental import pallas as pl
from jax.experimental.pallas import tpu as pltpu
from jax.sharding import Mesh, PartitionSpec as P

D = 8192
HID = 16384
TOKENS = 512
BF16 = jnp.bfloat16
F32 = jnp.float32
DP = ("yh", "zh", "zl", "c")
TP = ("yl", "x")
NEAR = ("c", "yl", "x")


def swap(x, axis):
    return lax.ppermute(x, axis, [(0, 1), (1, 0)])


def exchange(pieces, axes):
    return lax.all_to_all(pieces, axes, 0, 0, tiled=True)


def dot(a, b, dims=((1,), (0,))):
    return lax.dot_general(a, b, (dims, ((), ())), preferred_element_type=F32)


def local(kernel, outs, *args, scalars=0, after=0):
    spec = pl.BlockSpec(memory_space=pltpu.VMEM)
    small = pl.BlockSpec(memory_space=pltpu.SMEM)
    unread = pl.BlockSpec(memory_space=pl.ANY)
    return pl.pallas_call(
        kernel,
        out_shape=[jax.ShapeDtypeStruct(shape, dtype) for shape, dtype in outs],
        in_specs=[small] * scalars + [spec] * (len(args) - scalars - after) + [unread] * after,
        out_specs=[spec] * len(outs),
        compiler_params=pltpu.CompilerParams(vmem_limit_bytes=16 * 2**20),
    )(*args)


def copies_kernel(x_ref, o_ref):
    for i in range(o_ref.shape[0]):
        o_ref[i] = x_ref[...]


def keep(mask_ref, w_ref, o_ref):
    for i in range(mask_ref.shape[0]):
        for j in range(mask_ref.shape[1]):
            block = (slice(i * 128, (i + 1) * 128), slice(j * 128, (j + 1) * 128))
            o_ref[block] = (w_ref[block].astype(F32) * mask_ref[i, j].astype(F32)).astype(BF16)


def stack_kernel(gmask_ref, umask_ref, gate_ref, up_ref, pgate_ref, pup_ref, o_ref):
    width = gate_ref.shape[1]
    keep(gmask_ref, gate_ref, o_ref.at[:, :width])
    keep(umask_ref, up_ref, o_ref.at[:, width : 2 * width])
    o_ref[:, 2 * width : 3 * width] = pgate_ref[...]
    o_ref[:, 3 * width :] = pup_ref[...]


def pair_kernel(a_ref, b_ref, after_ref, after2_ref, o_ref):
    rows = a_ref.shape[0]
    o_ref[:rows] = a_ref[...]
    o_ref[rows:] = b_ref[...]


def hold_kernel(x_ref, after_ref, o_ref):
    o_ref[...] = x_ref[...]


def pre_kernel(own_ref, other_ref, w_ref, after_ref, o_ref, turned_ref):
    rows = own_ref.shape[0]
    turned_ref[:, :rows] = own_ref[...].T
    turned_ref[:, rows:] = other_ref[...].T
    width = w_ref.shape[1] // 4
    for half, tok_ref in enumerate((own_ref, other_ref)):
        for j in range(4):
            cols = slice(j * width, (j + 1) * width)
            y = dot(tok_ref[...], w_ref[:, cols]).astype(BF16)
            for r in range(2):
                q = 16 * (2 * half + r)
                o_ref[:, q : q + 16, cols] = y[r * 128 : (r + 1) * 128].reshape(8, 16, width)


def down_kernel(mask_ref, down_ref, probe_ref, o_ref):
    width = down_ref.shape[0]
    keep(mask_ref, down_ref, o_ref.at[:width, :])
    o_ref[width:, :] = probe_ref[...]


def gate_kernel(x_ref, o_ref, up_slope_ref, act_ref):
    width = act_ref.shape[1]

    def part(j):
        cols = slice(j * width, (j + 1) * width)
        acc = x_ref[0, :, cols].astype(F32)
        for i in range(1, 8):
            acc = acc + x_ref[i, :, cols].astype(F32)
        return acc

    gate = part(0)
    up = part(1)
    tangent_gate = part(2) * D**-0.5
    tangent_up = part(3) * D**-0.5
    sig = jax.nn.sigmoid(gate)
    act = gate * sig
    slope = sig * (1.0 + gate * (1.0 - sig))
    hid = (act * up).astype(BF16)
    tan = (slope * tangent_gate * up + act * tangent_up).astype(BF16)
    c = lax.axis_index("c")
    for r in range(2):
        rows = slice(r * 32, (r + 1) * 32)
        place = c if r == 0 else 1 - c
        for i in range(8):
            o_ref[place, i, :, :width] = tan[rows]
            o_ref[place, i, :, width:] = hid[rows]
    up_slope_ref[...] = up * slope
    act_ref[...] = act


def term_kernel(x_ref, down_ref, down2_ref, o_ref, hid_ref, hid2_ref):
    width = hid_ref.shape[1]
    c = lax.axis_index("c")
    yh = lax.axis_index("yh")

    def rows(src):
        parts = [x_ref[src, :, 16 * r : 16 * r + 16, :].reshape(128, 2 * width) for r in range(2)]
        return jnp.concatenate(parts, axis=0)

    own = rows(c)
    other = rows(1 - c)
    hid_ref[...] = own[:, width:]
    hid2_ref[...] = other[:, width:]
    for j in range(4):
        cols = slice(j * 256, (j + 1) * 256)
        y = dot(own[:, width:], down_ref[width:, cols]) + dot(other[:, width:], down2_ref[width:, cols])
        y = y * HID**-0.5
        y = y + dot(own[:, :width], down_ref[:width, cols])
        y = y + dot(other[:, :width], down2_ref[:width, cols])
        y = y.astype(BF16)
        for r in range(2):
            place = yh if r == 0 else 1 - yh
            o_ref[:, place, :, cols] = y[r * 128 : (r + 1) * 128].reshape(4, 32, 256)


def spread_kernel(x_ref, o_ref):
    acc = x_ref[0].astype(F32)
    for i in range(1, x_ref.shape[0]):
        acc = acc + x_ref[i].astype(F32)
    acc = acc.astype(BF16)
    for i in range(o_ref.shape[0]):
        o_ref[i] = acc


def back_kernel(x_ref, down_ref, down2_ref, o_ref, out_ref):
    width = o_ref.shape[3]
    c = lax.axis_index("c")
    yh = lax.axis_index("yh")
    for r in range(2):
        place = yh if r == 0 else 1 - yh
        out_ref[r * 128 : (r + 1) * 128, :] = x_ref[:, place].reshape(128, x_ref.shape[3])
    for w_ref, place in ((down_ref, c), (down2_ref, 1 - c)):
        y = dot(out_ref[...], w_ref[:width, :], ((1,), (1,))).astype(BF16)
        for r in range(2):
            o_ref[place, :, 16 * r : 16 * r + 16, :] = y[r * 128 : (r + 1) * 128].reshape(
                8, 16, width
            )


def bars_kernel(
    x_ref, up_slope_ref, act_ref, out_ref, hid2_ref, o_ref, late_ref, late2_ref, own_ref
):
    width = act_ref.shape[1]
    half = late_ref.shape[1]
    late_ref[...] = out_ref[:, :half]
    late2_ref[:, : half - width] = out_ref[:, half:]
    late2_ref[:, half - width :] = hid2_ref[...]
    own_ref[...] = out_ref[...]
    c = lax.axis_index("c")
    for r in range(2):
        place = c if r == 0 else 1 - c
        rows = slice(r * 32, (r + 1) * 32)
        back = x_ref[place, 0].astype(F32)
        for i in range(1, 8):
            back = back + x_ref[place, i].astype(F32)
        gate_bar = (back * up_slope_ref[rows]).astype(BF16)
        up_bar = (back * act_ref[rows]).astype(BF16)
        for i in range(8):
            o_ref[i, rows, :width] = gate_bar
            o_ref[i, rows, width:] = up_bar


def fisher_down_kernel(hid_ref, out_ref, late_ref, late2_ref, probe_ref, o_ref, done_ref):
    width = hid_ref.shape[1]
    half = late_ref.shape[1]
    rest = half - width
    own = hid_ref[...].T
    other = late2_ref[:, rest:].T
    for part_ref, start, count, column in (
        (late_ref, 0, rest, 0),
        (late_ref, rest, width, rest),
        (late2_ref, 0, rest, half),
    ):
        cols = slice(column, column + count)
        y = dot(own, out_ref[:, cols]) + dot(other, part_ref[:, start : start + count])
        o_ref[:, cols] = (probe_ref[:, cols].astype(F32) * y * TOKENS**-0.5).astype(BF16)
    done_ref[...] = late2_ref[:16, :128]


def fisher_kernel(tok_ref, bars_ref, probe_ref, after_ref, gate_ref, up_ref, g_ref, u_ref, sem):
    width = gate_ref.shape[1]
    factor = TOKENS**-0.5
    bars = [bars_ref[:, 16 * q : 16 * q + 16, :].reshape(128, 2 * width) for q in range(4)]
    bars = jnp.concatenate(bars, axis=0)
    writes = []
    for i in range(4):
        rows = slice(i * 256, (i + 1) * 256)
        y = dot(tok_ref[rows, :], bars)
        for j, (held, target) in enumerate(((g_ref, gate_ref), (u_ref, up_ref))):
            probe = probe_ref[rows, (2 + j) * width : (3 + j) * width].astype(F32)
            held[rows, :] = (probe * y[:, j * width : (j + 1) * width] * factor).astype(BF16)
            write = pltpu.make_async_copy(held.at[rows, :], target.at[rows, :], sem.at[i, j])
            write.start()
            writes.append(write)
    for write in writes:
        write.wait()


def fisher(tok, bars, stacked, after):
    rows = stacked.shape[0]
    width = stacked.shape[1] // 4
    spec = pl.BlockSpec(memory_space=pltpu.VMEM)
    unread = pl.BlockSpec(memory_space=pl.ANY)
    return pl.pallas_call(
        fisher_kernel,
        out_shape=[jax.ShapeDtypeStruct((rows, width), BF16)] * 2,
        in_specs=[spec, spec, spec, unread],
        out_specs=[unread, unread],
        scratch_shapes=[
            pltpu.VMEM((rows, width), BF16),
            pltpu.VMEM((rows, width), BF16),
            pltpu.SemaphoreType.DMA((4, 2)),
        ],
        compiler_params=pltpu.CompilerParams(vmem_limit_bytes=16 * 2**20),
    )(tok, bars, stacked, after)


def on_device(
    tokens,
    gate_weight,
    up_weight,
    down_weight,
    gate_mask,
    up_mask,
    down_mask,
    probe_gate,
    probe_up,
    probe_down,
):
    width = gate_weight.shape[1]
    feats = tokens.shape[1]

    (mine,) = local(copies_kernel, [((16, 8, feats), BF16)], tokens)
    tok0 = exchange(mine, ("zl", "zh")).reshape(128, feats)
    (stacked,) = local(
        stack_kernel,
        [((feats, 4 * width), BF16)],
        gate_mask,
        up_mask,
        gate_weight,
        up_weight,
        probe_gate,
        probe_up,
        scalars=2,
    )
    (down,) = local(
        down_kernel, [((2 * width, feats), BF16)], down_mask, down_weight, probe_down, scalars=1
    )
    down2 = swap(down, "c")
    tok1 = swap(tok0, "yh")
    (pair,) = local(pair_kernel, [((256, feats), BF16)], tok0, tok1, stacked, down2, after=2)
    pair2 = swap(pair, "c")
    (down2,) = local(hold_kernel, [(down2.shape, BF16)], down2, pair, after=1)
    partial, tok_t = local(
        pre_kernel,
        [((8, 64, 4 * width), BF16), ((feats, TOKENS), BF16)],
        pair,
        pair2,
        stacked,
        down2,
        after=1,
    )
    pre = exchange(partial, TP)
    send, up_slope, act = local(
        gate_kernel,
        [((2, 8, 32, 2 * width), BF16), ((64, width), F32), ((64, width), F32)],
        pre,
    )
    both = exchange(send.reshape(16, 32, 2 * width), NEAR).reshape(2, 8, 32, 2 * width)
    term, hid, hid2 = local(
        term_kernel,
        [((4, 2, 32, feats), BF16), ((256, width), BF16), ((256, width), BF16)],
        both,
        down,
        down2,
    )
    term = exchange(term.reshape(8, 32, feats), ("zl", "yh"))
    (chunk,) = local(spread_kernel, [((4, 32, feats), BF16)], term)
    chunk = exchange(chunk, "zh")
    (chunk,) = local(spread_kernel, [((8, 32, feats), BF16)], chunk)
    chunk = exchange(chunk, ("zl", "yh")).reshape(4, 2, 32, feats)
    back, out = local(
        back_kernel, [((2, 8, 32, width), BF16), ((256, feats), BF16)], chunk, down, down2
    )
    back = exchange(back.reshape(16, 32, width), NEAR).reshape(2, 8, 32, width)
    half = (feats + width) // 2
    bars, late, late2, out = local(
        bars_kernel,
        [
            ((8, 64, 2 * width), BF16),
            ((256, half), BF16),
            ((256, half), BF16),
            ((256, feats), BF16),
        ],
        back,
        up_slope,
        act,
        out,
        hid2,
    )
    bars = exchange(bars, TP)
    fisher_down, done = local(
        fisher_down_kernel,
        [(probe_down.shape, BF16), ((16, 128), BF16)],
        hid,
        out,
        swap(late, "c"),
        swap(late2, "c"),
        probe_down,
    )
    fisher_gate, fisher_up = fisher(tok_t, bars, stacked, done)
    return (fisher_gate, fisher_up, fisher_down)


def solution(mesh):
    fine = Mesh(mesh.devices.reshape(2, 4, 4, 2, 2, 4), DP + TP)
    col = P(TP, DP)
    row = P(DP, TP)
    return jax.shard_map(
        on_device,
        mesh=fine,
        in_specs=(row, col, col, row, col, col, row, col, col, row),
        out_specs=(col, col, row),
        check_vma=False,
    )
```
